256 devices in a mesh: gx: 16 (over y_hi, z), gy: 16 (over x, y_lo, core).
Axes of the slice: x: 4, y: 4 (y_hi: 2, y_lo: 2; y = y_hi * 2 + y_lo), z: 8, core: 2. Of those that a mesh axis runs over, the one named last changes fastest.
Arguments:
- velocity: float32 [3, 4, 128, 2048], P(None, None, 'gy', 'gx'), may hold values from -6 to 6
- old_lm: float32 [4, 128, 2048], P(None, 'gy', 'gx'), may hold values from -6 to 6
- old_mm: float32 [4, 128, 2048], P(None, 'gy', 'gx'), may hold values from 0.5 to 4
- offsets: int32 [3, 4, 128, 2048], P(None, None, 'gy', 'gx'), may hold values from -1 to 2, as said below
- fractions: float32 [3, 4, 128, 2048], P(None, None, 'gy', 'gx'), may hold values from 0 to 1
Outputs:
- new_lm: float32 [4, 128, 2048], P(None, 'gy', 'gx')
- new_mm: float32 [4, 128, 2048], P(None, 'gy', 'gx')
- coefficient: float32 [4, 128, 2048], P(None, 'gy', 'gx')
The draws below stay inside these ranges and needn't reach their ends.
Inputs may be any that keep to these rules, and one draw needn't show every extreme that they name: offsets[0] is the streamwise distance upstream, 0 or 1; offsets[1] is -1 or 0; offsets[2] is the cell's own level or the one below it, kept within 0 to 2.
All inputs are finite; a program needn't handle non-finite values.
Results may differ from the reference program's by a relative error of at most 0.000021.
Values sent between devices are 32-bit elements; how exact they have to be, the bound alone decides.
No kernel may reach another device: no remote copies, remote signals or barrier semaphores. Data moves between devices by JAX's collectives and lax.ppermute only.
A program may use at most 64 MiB of HBM per device.

```python
import math
import jax
import jax.numpy as jnp
from jax import lax

NZ = 4
NX = 2048
NY = 128


def draw_offsets(key, part):
    key = jax.random.fold_in(key, 5)
    key_stream, key_span, key_level = jax.random.split(key, 3)
    streamwise = jax.random.randint(key_stream, (NZ, NY, NX), 0, 2)
    spanwise = jax.random.randint(key_span, (NZ, NY, NX), -1, 1)
    below = jax.random.randint(key_level, (NZ, NY, NX), 0, 2)
    heights = jnp.arange(NZ, dtype=jnp.int32)[:, None, None]
    level = jnp.clip(heights - below, 0, NZ - 2)
    return jnp.stack([streamwise, spanwise, level]).astype(jnp.int32)


def level_of(rng, shape, cuts, low, largest):
    gain = 1.0
    for axis_at, blocks in cuts:
        draws = jax.random.uniform(jax.random.fold_in(jax.random.fold_in(rng, 6), axis_at), (blocks,), jnp.float32, low / len(cuts), largest / len(cuts))
        gain = gain * jnp.repeat(jnp.exp(draws), shape[axis_at] // blocks).reshape((-1,) + (1,) * (len(shape) - 1 - axis_at))
    return gain


def gaussian(own_key, shape, width, most, cuts=(), held_as=jnp.bfloat16):
    entries = width * jax.random.normal(own_key, shape, jnp.float32)
    if cuts:
        entries = entries * level_of(own_key, shape, cuts, -0.22, 0.18)
    return jnp.clip(entries, -most, most).astype(held_as)


def setup_inputs(seed: int = 0) -> dict:
    streams_of = jax.random.split(jax.random.key(seed), 6)
    velocity = gaussian(streams_of[0], (3, NZ, NY, NX), 1.0, 6.0, ((2, 16), (3, 16)), jnp.float32)
    old_lm = gaussian(streams_of[1], (NZ, NY, NX), 1.0, 6.0, ((1, 16), (2, 16)), jnp.float32)
    old_mm = jnp.clip(jnp.exp(math.log(4.0) - 2.0794415 * jax.random.uniform(streams_of[2], (NZ, NY, NX), jnp.float32) ** level_of(streams_of[2], (NZ, NY, NX), ((1, 16), (2, 16)), -0.2, 0.2)), 0.5, 4.0)
    offsets = draw_offsets(jax.random.fold_in(streams_of[5], 71), 0)
    fractions = jnp.clip(1.0 * jax.random.uniform(streams_of[4], (3, NZ, NY, NX), jnp.float32) ** level_of(streams_of[4], (3, NZ, NY, NX), ((2, 16), (3, 16)), -0.2, 0.2), 0.0, 1.0)
    return dict(velocity=velocity, old_lm=old_lm, old_mm=old_mm, offsets=offsets, fractions=fractions)


relax_rate = 0.3
filter_area = 0.63
spacing_z = 0.5
PAIR_FIRST = (0, 1, 2, 0, 0, 1)
PAIR_SECOND = (0, 1, 2, 1, 2, 2)
PAIR_WEIGHT = (1.0, 1.0, 1.0, 2.0, 2.0, 2.0)

def vertical_slope(field):
    inner = (field[..., 2:, :, :] - field[..., :-2, :, :]) * (0.5 / spacing_z)
    bottom = (field[..., 1:2, :, :] - field[..., 0:1, :, :]) * (1.0 / spacing_z)
    top = (field[..., -1:, :, :] - field[..., -2:-1, :, :]) * (1.0 / spacing_z)
    return jnp.concatenate([bottom, inner, top], axis=-3)

def smooth(field):
    along = 0.25 * jnp.roll(field, 1, -1) + 0.5 * field + 0.25 * jnp.roll(field, -1, -1)
    return 0.25 * jnp.roll(along, 1, -2) + 0.5 * along + 0.25 * jnp.roll(along, -1, -2)

def slopes(field):
    ddx_part = (jnp.roll(field, -1, -1) - jnp.roll(field, 1, -1)) * 0.5
    ddy_part = (jnp.roll(field, -1, -2) - jnp.roll(field, 1, -2)) * 0.5
    return (ddx_part, ddy_part, vertical_slope(field))

def strain_parts(gradient):
    parts = jnp.stack([0.5 * (gradient[second][first] + gradient[first][second]) for first, second in zip(PAIR_FIRST, PAIR_SECOND)])
    weights = jnp.array(PAIR_WEIGHT, jnp.float32).reshape(6, 1, 1, 1)
    magnitude = jnp.sqrt(2.0 * lax.optimization_barrier(jnp.sum(weights * parts * parts, axis=0)))
    return (parts, magnitude)

def contract(filtered_products, filtered_vel, filtered_model, strain_f, magnitude_f):
    weights = jnp.array(PAIR_WEIGHT, jnp.float32).reshape(6, 1, 1, 1)
    resolved = filtered_products - jnp.stack([filtered_vel[first] * filtered_vel[second] for first, second in zip(PAIR_FIRST, PAIR_SECOND)])
    modelled = 2.0 * filter_area * (filtered_model - 4.0 * magnitude_f[None] * strain_f)
    germano_lm = lax.optimization_barrier(jnp.sum(weights * resolved * modelled, axis=0))
    germano_mm = lax.optimization_barrier(jnp.sum(weights * modelled * modelled, axis=0))
    return (germano_lm, germano_mm)

def interpolate(old_lm, old_mm, offsets, fractions):
    stacked = jnp.stack([old_lm, old_mm]).reshape(2, -1)
    col_x = jnp.arange(NX, dtype=jnp.int32)[None, None, :]
    row_y = jnp.arange(NY, dtype=jnp.int32)[None, :, None]
    base_x = jnp.mod(col_x - offsets[0], NX)
    base_y = jnp.mod(row_y + offsets[1], NY)
    level = offsets[2]
    total = jnp.zeros((2, NZ, NY, NX), jnp.float32)
    for step_z in (0, 1):
        for step_y in (0, 1):
            for step_x in (0, 1):
                weight_x = fractions[0] if step_x else 1.0 - fractions[0]
                weight_y = fractions[1] if step_y else 1.0 - fractions[1]
                weight_z = fractions[2] if step_z else 1.0 - fractions[2]
                weight = weight_x * weight_y * weight_z
                flat = ((level + step_z) * NY + jnp.mod(base_y + step_y, NY)) * NX + jnp.mod(base_x + step_x, NX)
                picked = jnp.take(stacked, flat.reshape(-1).astype(jnp.int32), axis=1).reshape(2, NZ, NY, NX)
                total = total + weight[None] * picked
    return total

def reference(velocity, old_lm, old_mm, offsets, fractions):
    products = jnp.stack([velocity[first] * velocity[second] for first, second in zip(PAIR_FIRST, PAIR_SECOND)])
    filtered_products = smooth(products)
    filtered_vel = smooth(velocity)
    strain, magnitude = strain_parts(slopes(velocity))
    filtered_model = smooth(magnitude[None] * strain)
    strain_f, magnitude_f = strain_parts(slopes(filtered_vel))
    germano_lm, germano_mm = contract(filtered_products, filtered_vel, filtered_model, strain_f, magnitude_f)
    carried = interpolate(old_lm, old_mm, offsets, fractions)
    new_lm = relax_rate * germano_lm + (1.0 - relax_rate) * carried[0]
    new_mm = relax_rate * germano_mm + (1.0 - relax_rate) * carried[1]
    coefficient = jnp.maximum(new_lm, 0.0) / new_mm
    return (new_lm, new_mm, coefficient)
```

```python
import functools

import jax
import jax.numpy as jnp
from jax import lax
from jax.experimental import pallas as pl
from jax.experimental.pallas import tpu as pltpu
from jax.sharding import PartitionSpec as P

relax_rate = 0.3
filter_area = 0.63
spacing_z = 0.5
PAIR_FIRST = (0, 1, 2, 0, 0, 1)
PAIR_SECOND = (0, 1, 2, 1, 2, 2)
LEVELS = 4
ROWS = 8
COLS = 128
PLANES = 3 * LEVELS
OLD = 2 * LEVELS
VMEM = pl.BlockSpec(memory_space=pltpu.VMEM)


def edge_shift(plane):
    return 4 * plane if plane < PLANES else 4 * PLANES + 2 * (plane - PLANES)


def right_mask():
    lane = lax.broadcasted_iota(jnp.int32, (ROWS, COLS), 1)
    step = jnp.where(lane < 4 * PLANES - 2, lane % 4, 2 * (lane % 2))
    return (step < 2) & (lane < 4 * PLANES + 2 * OLD)


def packed_edges(tiles):
    lane = lax.broadcasted_iota(jnp.int32, (ROWS, COLS), 1)
    packed = tiles[0]
    for plane in range(1, PLANES + OLD):
        at = edge_shift(plane)
        first = at - (2 if plane < PLANES else 1)
        packed = jnp.where(lane >= first, pltpu.roll(tiles[plane], at, 1), packed)
    last = edge_shift(0) + COLS - 2
    return jnp.where(lane >= last, tiles[0], packed)


def pack_kernel(vel, old_lm, old_mm, msg_a, msg_b, edges):
    even = 1 - lax.axis_index("gy") % 2
    tiles = []
    for plane in range(PLANES):
        ref = vel.at[plane // LEVELS, plane % LEVELS]
        tiles.append(ref[...])
        msg_a[2 * plane : 2 * plane + 2, :] = ref[pl.ds(6 * even, 2), :]
        msg_b[2 * plane : 2 * plane + 2, :] = ref[pl.ds(6 - 6 * even, 2), :]
    for plane in range(OLD):
        ref = (old_lm, old_mm)[plane // LEVELS].at[plane % LEVELS]
        tiles.append(ref[...])
        msg_a[2 * PLANES + plane : 2 * PLANES + plane + 1, :] = ref[pl.ds(7 * even, 1), :]
        msg_b[2 * PLANES + plane : 2 * PLANES + plane + 1, :] = ref[pl.ds(7 - 7 * even, 1), :]
    edges[...] = packed_edges(tiles)


def rows_kernel(got_a, got_b, own_edges, outer, edges):
    even = lax.axis_index("gy") % 2 == 0
    above = jnp.where(even, got_a[...], got_b[...])
    below = jnp.where(even, got_b[...], got_a[...])
    outer[...] = jnp.zeros_like(outer)
    for plane in range(PLANES):
        outer[plane, 0:2, :] = above[2 * plane : 2 * plane + 2]
        outer[plane, 6:8, :] = below[2 * plane : 2 * plane + 2]
    for plane in range(PLANES, PLANES + OLD):
        outer[plane, 0:1, :] = above[PLANES + plane : PLANES + plane + 1]
        outer[plane, 7:8, :] = below[PLANES + plane : PLANES + plane + 1]
    edges[0:ROWS, :] = own_edges[...]
    edges[ROWS:, :] = packed_edges([outer[plane] for plane in range(PLANES + OLD)])


class Shifts:
    def __init__(self):
        shape = (LEVELS, ROWS, COLS)
        lane = lax.broadcasted_iota(jnp.int32, shape, 2)
        row = lax.broadcasted_iota(jnp.int32, shape, 1)
        self.lane_first, self.lane_last = lane == 0, lane == COLS - 1
        self.row_first, self.row_last = row == 0, row == ROWS - 1

    def east(self, here, other):
        return pltpu.roll(jnp.where(self.lane_first, other, here), COLS - 1, 2)

    def west(self, here, other):
        return pltpu.roll(jnp.where(self.lane_last, other, here), 1, 2)

    def north(self, here, other):
        return pltpu.roll(jnp.where(self.row_first, other, here), ROWS - 1, 1)

    def south(self, here, other):
        return pltpu.roll(jnp.where(self.row_last, other, here), 1, 1)


def weighted(low, mid, high):
    return 0.25 * low + 0.5 * mid + 0.25 * high


def vertical_slope(field):
    inner = (field[2:] - field[:-2]) * (0.5 / spacing_z)
    bottom = (field[1:2] - field[0:1]) * (1.0 / spacing_z)
    top = (field[-1:] - field[-2:-1]) * (1.0 / spacing_z)
    return jnp.concatenate([bottom, inner, top], axis=0)


def strain_parts(gradient):
    parts = [
        gradient[a][a] if a == b else 0.5 * (gradient[b][a] + gradient[a][b])
        for a, b in zip(PAIR_FIRST, PAIR_SECOND)
    ]
    total = parts[0] * parts[0] + parts[1] * parts[1] + parts[2] * parts[2]
    cross = parts[3] * parts[3] + parts[4] * parts[4] + parts[5] * parts[5]
    return parts, jnp.sqrt(2.0 * (total + 2.0 * cross))


def main_kernel(
    vel, old_lm, old_mm, offsets, fractions, outer, edges_a, edges_b, new_lm, new_mm, coefficient
):
    sh = Shifts()
    even = lax.axis_index("gx") % 2 == 0
    right = right_mask()
    halves = []
    for half in range(2):
        a = edges_a[half * ROWS : (half + 1) * ROWS, :]
        b = edges_b[half * ROWS : (half + 1) * ROWS, :]
        halves.append(jnp.where(even, jnp.where(right, a, b), jnp.where(right, b, a)))

    def four(first_plane, own):
        side = [
            jnp.stack(
                [
                    pltpu.roll(half, (COLS - edge_shift(first_plane + z)) % COLS, 1)
                    for z in range(LEVELS)
                ]
            )
            for half in halves
        ]
        return own, side[0], outer[first_plane : first_plane + LEVELS], side[1]

    fields = [four(LEVELS * c, vel[c]) for c in range(3)]
    west, east, along = [], [], []
    for tiles in fields:
        own, side, rows, corner = tiles
        west.append([sh.west(own, side), sh.west(side, own), sh.west(rows, corner), sh.west(corner, rows)])
        east.append([sh.east(own, side), sh.east(side, own), sh.east(rows, corner), sh.east(corner, rows)])
        along.append([weighted(west[-1][t], tiles[t], east[-1][t]) for t in range(4)])
    filtered = []
    for c in range(3):
        filtered.append(
            [
                weighted(sh.south(along[c][t], along[c][t ^ 2]), along[c][t], sh.north(along[c][t], along[c][t ^ 2]))
                for t in range(4)
            ]
        )
    modelled = []
    for t in range(4):
        gradient = [
            (
                0.5 * (east[c][t] - west[c][t]),
                0.5 * (sh.north(fields[c][t], fields[c][t ^ 2]) - sh.south(fields[c][t], fields[c][t ^ 2])),
                vertical_slope(fields[c][t]),
            )
            for c in range(3)
        ]
        parts, magnitude = strain_parts(gradient)
        modelled.append([magnitude * part for part in parts])
    own = [filtered[c][0] for c in range(3)]
    gradient = []
    for c in range(3):
        f, side, rows, _ = filtered[c]
        gradient.append(
            (
                0.5 * (sh.east(f, side) - sh.west(f, side)),
                0.5 * (sh.north(f, rows) - sh.south(f, rows)),
                vertical_slope(f),
            )
        )
    parts_f, magnitude_f = strain_parts(gradient)
    lm = mm = 0.0
    for pair, (a, b) in enumerate(zip(PAIR_FIRST, PAIR_SECOND)):
        line, model = [], []
        for t in (0, 2):
            line.append(
                weighted(west[a][t] * west[b][t], fields[a][t] * fields[b][t], east[a][t] * east[b][t])
            )
            here, side = modelled[t][pair], modelled[t + 1][pair]
            model.append(weighted(sh.west(here, side), here, sh.east(here, side)))
        product = weighted(sh.south(*line), line[0], sh.north(*line))
        smooth = weighted(sh.south(*model), model[0], sh.north(*model))
        resolved = product - own[a] * own[b]
        m = 2.0 * filter_area * (smooth - 4.0 * magnitude_f * parts_f[pair])
        weight = 1.0 if a == b else 2.0
        lm = lm + weight * resolved * m
        mm = mm + weight * m * m

    upstream = offsets[0] == 1
    f0, f1, f2 = fractions[0], fractions[1], fractions[2]
    back = offsets[1] == -1
    g0, g1, g2 = 1.0 - f0, 1.0 - f1, 1.0 - f2
    wx = (jnp.where(upstream, g0, 0.0), jnp.where(upstream, f0, g0), jnp.where(upstream, 0.0, f0))
    wy = (jnp.where(back, g1, 0.0), jnp.where(back, f1, g1), jnp.where(back, 0.0, f1))
    level = offsets[2]
    carried = []
    for k, ref in enumerate((old_lm, old_mm)):
        here, side, rows, corner = four(PLANES + LEVELS * k, ref[...])
        columns = [
            (sh.west(here, side), sh.west(rows, corner)),
            (here, rows),
            (sh.east(here, side), sh.east(rows, corner)),
        ]
        nine = [[sh.south(*pair), pair[0], sh.north(*pair)] for pair in columns]
        total = []
        for z in range(LEVELS):
            value = 0.0
            for s in range(max(z - 1, 0), min(z + 2, LEVELS)):
                weight = jnp.where(level[z] == s, g2[z], jnp.where(level[z] == s - 1, f2[z], 0.0))
                plane = 0.0
                for y in range(3):
                    row = wx[0][z] * nine[0][y][s] + wx[1][z] * nine[1][y][s] + wx[2][z] * nine[2][y][s]
                    plane = plane + wy[y][z] * row
                value = value + weight * plane
            total.append(value)
        carried.append(jnp.stack(total))
    lm_out = relax_rate * lm + (1.0 - relax_rate) * carried[0]
    mm_out = relax_rate * mm + (1.0 - relax_rate) * carried[1]
    new_lm[...] = lm_out
    new_mm[...] = mm_out
    coefficient[...] = jnp.maximum(lm_out, 0.0) / mm_out


def f32(*shape):
    return jax.ShapeDtypeStruct(shape, jnp.float32)


def kernel_call(kernel, outs, args):
    return pl.pallas_call(
        kernel,
        out_shape=outs,
        in_specs=[VMEM] * len(args),
        out_specs=[VMEM] * len(outs),
        compiler_params=pltpu.CompilerParams(vmem_limit_bytes=16 * 1024 * 1024),
    )(*args)


def even_pairs(count):
    return [(i, i ^ 1) for i in range(count)]


def odd_pairs(count):
    return [(i, (((i + 1) % count ^ 1) - 1) % count) for i in range(count)]


def body(velocity, old_lm, old_mm, offsets, fractions):
    nx, ny = lax.axis_size("gx"), lax.axis_size("gy")
    rows = 2 * PLANES + OLD
    msg_a, msg_b, own_edges = kernel_call(
        pack_kernel, [f32(rows, COLS), f32(rows, COLS), f32(ROWS, COLS)], (velocity, old_lm, old_mm)
    )
    got_a = lax.ppermute(msg_a, "gy", even_pairs(ny))
    got_b = lax.ppermute(msg_b, "gy", odd_pairs(ny))
    outer, edges = kernel_call(
        rows_kernel, [f32(PLANES + OLD, ROWS, COLS), f32(2 * ROWS, COLS)], (got_a, got_b, own_edges)
    )
    edges_a = lax.ppermute(edges, "gx", even_pairs(nx))
    edges_b = lax.ppermute(edges, "gx", odd_pairs(nx))
    out = f32(LEVELS, ROWS, COLS)
    return tuple(
        kernel_call(
            main_kernel,
            [out, out, out],
            (velocity, old_lm, old_mm, offsets, fractions, outer, edges_a, edges_b),
        )
    )


def solution(mesh):
    placed = (
        P(None, None, "gy", "gx"),
        P(None, "gy", "gx"),
        P(None, "gy", "gx"),
        P(None, None, "gy", "gx"),
        P(None, None, "gy", "gx"),
    )
    return jax.shard_map(
        body,
        mesh=mesh,
        in_specs=placed,
        out_specs=(P(None, "gy", "gx"), P(None, "gy", "gx"), P(None, "gy", "gx")),
        check_vma=False,
    )
```

```python
import functools

import jax
import jax.numpy as jnp
from jax import lax
from jax.experimental import pallas as pl
from jax.experimental.pallas import tpu as pltpu
from jax.sharding import PartitionSpec as P

relax_rate = 0.3
filter_area = 0.63
spacing_z = 0.5
PAIR_FIRST = (0, 1, 2, 0, 0, 1)
PAIR_SECOND = (0, 1, 2, 1, 2, 2)
LEVELS = 4
ROWS = 8
COLS = 128
PLANES = 3 * LEVELS
OLD = 2 * LEVELS
VMEM = pl.BlockSpec(memory_space=pltpu.VMEM)
HBM = pl.BlockSpec(memory_space=pltpu.HBM)


def edge_shift(plane):
    return 4 * plane if plane < PLANES else 4 * PLANES + 2 * (plane - PLANES)


def right_mask():
    lane = lax.broadcasted_iota(jnp.int32, (ROWS, COLS), 1)
    step = jnp.where(lane < 4 * PLANES - 2, lane % 4, 2 * (lane % 2))
    return (step < 2) & (lane < 4 * PLANES + 2 * OLD)


def packed_edges(tiles):
    lane = lax.broadcasted_iota(jnp.int32, (ROWS, COLS), 1)
    packed = tiles[0]
    for plane in range(1, PLANES + OLD):
        at = edge_shift(plane)
        first = at - (2 if plane < PLANES else 1)
        packed = jnp.where(lane >= first, pltpu.roll(tiles[plane], at, 1), packed)
    last = edge_shift(0) + COLS - 2
    return jnp.where(lane >= last, tiles[0], packed)


def pack_kernel(
    vel_hbm, lm_hbm, mm_hbm, msg_a, msg_b, edges, vel, old, sems
):
    pairs = ((vel_hbm, vel), (lm_hbm, old.at[0]), (mm_hbm, old.at[1]))
    copies = [pltpu.make_async_copy(*pair, sems.at[k]) for k, pair in enumerate(pairs)]
    for copy in copies:
        copy.start()
    even = 1 - lax.axis_index("gy") % 2
    for copy in copies[:3]:
        copy.wait()
    tiles = []
    for plane in range(PLANES):
        ref = vel.at[plane // LEVELS, plane % LEVELS]
        tiles.append(ref[...])
        msg_a[2 * plane : 2 * plane + 2, :] = ref[pl.ds(6 * even, 2), :]
        msg_b[2 * plane : 2 * plane + 2, :] = ref[pl.ds(6 - 6 * even, 2), :]
    for plane in range(OLD):
        ref = old.at[plane // LEVELS, plane % LEVELS]
        tiles.append(ref[...])
        at = 2 * PLANES + plane
        msg_a[at : at + 1, :] = ref[pl.ds(7 * even, 1), :]
        msg_b[at : at + 1, :] = ref[pl.ds(7 - 7 * even, 1), :]
    edges[...] = packed_edges(tiles)


def hold_kernel(off_hbm, frac_hbm, _, off, frac, sems):
    copies = [
        pltpu.make_async_copy(off_hbm, off, sems.at[0]),
        pltpu.make_async_copy(frac_hbm, frac, sems.at[1]),
    ]
    for copy in copies:
        copy.start()
    for copy in copies:
        copy.wait()


def rows_kernel(got_a, got_b, own_edges, outer, edges):
    even = lax.axis_index("gy") % 2 == 0
    above = jnp.where(even, got_a[...], got_b[...])
    below = jnp.where(even, got_b[...], got_a[...])
    outer[...] = jnp.zeros_like(outer)
    for plane in range(PLANES):
        outer[plane, 0:2, :] = above[2 * plane : 2 * plane + 2]
        outer[plane, 6:8, :] = below[2 * plane : 2 * plane + 2]
    for plane in range(PLANES, PLANES + OLD):
        outer[plane, 0:1, :] = above[PLANES + plane : PLANES + plane + 1]
        outer[plane, 7:8, :] = below[PLANES + plane : PLANES + plane + 1]
    edges[0:ROWS, :] = own_edges[...]
    edges[ROWS:, :] = packed_edges([outer[plane] for plane in range(PLANES + OLD)])


class Shifts:
    def __init__(self):
        shape = (LEVELS, ROWS, COLS)
        lane = lax.broadcasted_iota(jnp.int32, shape, 2)
        row = lax.broadcasted_iota(jnp.int32, shape, 1)
        self.lane_first, self.lane_last = lane == 0, lane == COLS - 1
        self.row_first, self.row_last = row == 0, row == ROWS - 1

    def east(self, here, other):
        return pltpu.roll(jnp.where(self.lane_first, other, here), COLS - 1, 2)

    def west(self, here, other):
        return pltpu.roll(jnp.where(self.lane_last, other, here), 1, 2)

    def north(self, here, other):
        return pltpu.roll(jnp.where(self.row_first, other, here), ROWS - 1, 1)

    def south(self, here, other):
        return pltpu.roll(jnp.where(self.row_last, other, here), 1, 1)


def weighted(low, mid, high):
    return 0.25 * low + 0.5 * mid + 0.25 * high


def vertical_slope(field):
    inner = (field[2:] - field[:-2]) * (0.5 / spacing_z)
    bottom = (field[1:2] - field[0:1]) * (1.0 / spacing_z)
    top = (field[-1:] - field[-2:-1]) * (1.0 / spacing_z)
    return jnp.concatenate([bottom, inner, top], axis=0)


def strain_parts(gradient):
    parts = [
        gradient[a][a] if a == b else 0.5 * (gradient[b][a] + gradient[a][b])
        for a, b in zip(PAIR_FIRST, PAIR_SECOND)
    ]
    total = parts[0] * parts[0] + parts[1] * parts[1] + parts[2] * parts[2]
    cross = parts[3] * parts[3] + parts[4] * parts[4] + parts[5] * parts[5]
    return parts, jnp.sqrt(2.0 * (total + 2.0 * cross))


def main_kernel(
    vel, old_lm, old_mm, offsets, fractions, outer, edges_a, edges_b, new_lm, new_mm, coefficient
):
    sh = Shifts()
    even = lax.axis_index("gx") % 2 == 0
    right = right_mask()
    halves = []
    for half in range(2):
        a = edges_a[half * ROWS : (half + 1) * ROWS, :]
        b = edges_b[half * ROWS : (half + 1) * ROWS, :]
        halves.append(jnp.where(even, jnp.where(right, a, b), jnp.where(right, b, a)))

    def four(first_plane, own):
        side = [
            jnp.stack(
                [
                    pltpu.roll(half, (COLS - edge_shift(first_plane + z)) % COLS, 1)
                    for z in range(LEVELS)
                ]
            )
            for half in halves
        ]
        return own, side[0], outer[first_plane : first_plane + LEVELS], side[1]

    fields = [four(LEVELS * c, vel[c]) for c in range(3)]
    west, east, along = [], [], []
    for tiles in fields:
        own, side, rows, corner = tiles
        west.append([sh.west(own, side), sh.west(side, own), sh.west(rows, corner), sh.west(corner, rows)])
        east.append([sh.east(own, side), sh.east(side, own), sh.east(rows, corner), sh.east(corner, rows)])
        along.append([weighted(west[-1][t], tiles[t], east[-1][t]) for t in range(4)])
    filtered = []
    for c in range(3):
        filtered.append(
            [
                weighted(sh.south(along[c][t], along[c][t ^ 2]), along[c][t], sh.north(along[c][t], along[c][t ^ 2]))
                for t in range(4)
            ]
        )
    modelled = []
    for t in range(4):
        gradient = [
            (
                0.5 * (east[c][t] - west[c][t]),
                0.5 * (sh.north(fields[c][t], fields[c][t ^ 2]) - sh.south(fields[c][t], fields[c][t ^ 2])),
                vertical_slope(fields[c][t]),
            )
            for c in range(3)
        ]
        parts, magnitude = strain_parts(gradient)
        modelled.append([magnitude * part for part in parts])
    own = [filtered[c][0] for c in range(3)]
    gradient = []
    for c in range(3):
        f, side, rows, _ = filtered[c]
        gradient.append(
            (
                0.5 * (sh.east(f, side) - sh.west(f, side)),
                0.5 * (sh.north(f, rows) - sh.south(f, rows)),
                vertical_slope(f),
            )
        )
    parts_f, magnitude_f = strain_parts(gradient)
    lm = mm = 0.0
    for pair, (a, b) in enumerate(zip(PAIR_FIRST, PAIR_SECOND)):
        line, model = [], []
        for t in (0, 2):
            line.append(
                weighted(west[a][t] * west[b][t], fields[a][t] * fields[b][t], east[a][t] * east[b][t])
            )
            here, side = modelled[t][pair], modelled[t + 1][pair]
            model.append(weighted(sh.west(here, side), here, sh.east(here, side)))
        product = weighted(sh.south(*line), line[0], sh.north(*line))
        smooth = weighted(sh.south(*model), model[0], sh.north(*model))
        resolved = product - own[a] * own[b]
        m = 2.0 * filter_area * (smooth - 4.0 * magnitude_f * parts_f[pair])
        weight = 1.0 if a == b else 2.0
        lm = lm + weight * resolved * m
        mm = mm + weight * m * m

    upstream = offsets[0] == 1
    f0, f1, f2 = fractions[0], fractions[1], fractions[2]
    back = offsets[1] == -1
    g0, g1, g2 = 1.0 - f0, 1.0 - f1, 1.0 - f2
    wx = (jnp.where(upstream, g0, 0.0), jnp.where(upstream, f0, g0), jnp.where(upstream, 0.0, f0))
    wy = (jnp.where(back, g1, 0.0), jnp.where(back, f1, g1), jnp.where(back, 0.0, f1))
    level = offsets[2]
    carried = []
    for k, ref in enumerate((old_lm, old_mm)):
        here, side, rows, corner = four(PLANES + LEVELS * k, ref[...])
        columns = [
            (sh.west(here, side), sh.west(rows, corner)),
            (here, rows),
            (sh.east(here, side), sh.east(rows, corner)),
        ]
        nine = [[sh.south(*pair), pair[0], sh.north(*pair)] for pair in columns]
        total = []
        for z in range(LEVELS):
            value = 0.0
            for s in range(max(z - 1, 0), min(z + 2, LEVELS)):
                weight = jnp.where(level[z] == s, g2[z], jnp.where(level[z] == s - 1, f2[z], 0.0))
                plane = 0.0
                for y in range(3):
                    row = wx[0][z] * nine[0][y][s] + wx[1][z] * nine[1][y][s] + wx[2][z] * nine[2][y][s]
                    plane = plane + wy[y][z] * row
                value = value + weight * plane
            total.append(value)
        carried.append(jnp.stack(total))
    lm_out = relax_rate * lm + (1.0 - relax_rate) * carried[0]
    mm_out = relax_rate * mm + (1.0 - relax_rate) * carried[1]
    new_lm[...] = lm_out
    new_mm[...] = mm_out
    coefficient[...] = jnp.maximum(lm_out, 0.0) / mm_out


def f32(*shape):
    return jax.ShapeDtypeStruct(shape, jnp.float32)


def kernel_call(kernel, outs, args, space=VMEM, scratch=(), limit=16 * 1024):
    return pl.pallas_call(
        kernel,
        out_shape=outs,
        in_specs=[space] * len(args) if isinstance(space, pl.BlockSpec) else space,
        out_specs=[VMEM] * len(outs),
        scratch_shapes=scratch,
        compiler_params=pltpu.CompilerParams(vmem_limit_bytes=limit * 1024),
    )(*args)


def even_pairs(count):
    return [(i, i ^ 1) for i in range(count)]


def odd_pairs(count):
    return [(i, (((i + 1) % count ^ 1) - 1) % count) for i in range(count)]


def body(velocity, old_lm, old_mm, offsets, fractions):
    nx, ny = lax.axis_size("gx"), lax.axis_size("gy")
    rows = 2 * PLANES + OLD
    msg_a, msg_b, own_edges = kernel_call(
        pack_kernel,
        [f32(rows, COLS), f32(rows, COLS), f32(ROWS, COLS)],
        (velocity, old_lm, old_mm),
        space=HBM,
        scratch=[
            pltpu.VMEM((3, LEVELS, ROWS, COLS), jnp.float32),
            pltpu.VMEM((2, LEVELS, ROWS, COLS), jnp.float32),
            pltpu.SemaphoreType.DMA((3,)),
        ],
        limit=55190,
    )
    got_a = lax.ppermute(msg_a, "gy", even_pairs(ny))
    got_b = lax.ppermute(msg_b, "gy", odd_pairs(ny))
    offsets, fractions = kernel_call(
        hold_kernel,
        [jax.ShapeDtypeStruct(offsets.shape, offsets.dtype), f32(3, LEVELS, ROWS, COLS)],
        (offsets, fractions, own_edges),
        space=[HBM, HBM, VMEM],
        scratch=[pltpu.SemaphoreType.DMA((2,))],
        limit=55116,
    )
    outer, edges = kernel_call(
        rows_kernel, [f32(PLANES + OLD, ROWS, COLS), f32(2 * ROWS, COLS)], (got_a, got_b, own_edges)
    )
    edges_a = lax.ppermute(edges, "gx", even_pairs(nx))
    edges_b = lax.ppermute(edges, "gx", odd_pairs(nx))
    out = f32(LEVELS, ROWS, COLS)
    return tuple(
        kernel_call(
            main_kernel,
            [out, out, out],
            (velocity, old_lm, old_mm, offsets, fractions, outer, edges_a, edges_b),
        )
    )


def solution(mesh):
    placed = (
        P(None, None, "gy", "gx"),
        P(None, "gy", "gx"),
        P(None, "gy", "gx"),
        P(None, None, "gy", "gx"),
        P(None, None, "gy", "gx"),
    )
    return jax.shard_map(
        body,
        mesh=mesh,
        in_specs=placed,
        out_specs=(P(None, "gy", "gx"), P(None, "gy", "gx"), P(None, "gy", "gx")),
        check_vma=False,
    )
```

```python
import functools

import jax
import jax.numpy as jnp
from jax import lax
from jax.experimental import pallas as pl
from jax.experimental.pallas import tpu as pltpu
from jax.sharding import PartitionSpec as P

relax_rate = 0.3
filter_area = 0.63
spacing_z = 0.5
PAIR_FIRST = (0, 1, 2, 0, 0, 1)
PAIR_SECOND = (0, 1, 2, 1, 2, 2)
LEVELS = 4
ROWS = 8
COLS = 128
PLANES = 3 * LEVELS
OLD = 2 * LEVELS
VMEM = pl.BlockSpec(memory_space=pltpu.VMEM)
HBM = pl.BlockSpec(memory_space=pltpu.HBM)


def edge_shift(plane):
    return 4 * plane if plane < PLANES else 4 * PLANES + 2 * (plane - PLANES)


def right_mask():
    lane = lax.broadcasted_iota(jnp.int32, (ROWS, COLS), 1)
    step = jnp.where(lane < 4 * PLANES - 2, lane % 4, 2 * (lane % 2))
    return (step < 2) & (lane < 4 * PLANES + 2 * OLD)


def packed_edges(tiles):
    lane = lax.broadcasted_iota(jnp.int32, (ROWS, COLS), 1)
    packed = tiles[0]
    for plane in range(1, PLANES + OLD):
        at = edge_shift(plane)
        first = at - (2 if plane < PLANES else 1)
        packed = jnp.where(lane >= first, pltpu.roll(tiles[plane], at, 1), packed)
    last = edge_shift(0) + COLS - 2
    return jnp.where(lane >= last, tiles[0], packed)


def pack_kernel(
    vel_hbm, lm_hbm, mm_hbm, msg_a, msg_b, edges, vel, old, sems
):
    pairs = ((vel_hbm, vel), (lm_hbm, old.at[0]), (mm_hbm, old.at[1]))
    copies = [pltpu.make_async_copy(*pair, sems.at[k]) for k, pair in enumerate(pairs)]
    for copy in copies:
        copy.start()
    even = 1 - lax.axis_index("gy") % 2
    for copy in copies[:3]:
        copy.wait()
    tiles = []
    for plane in range(PLANES):
        ref = vel.at[plane // LEVELS, plane % LEVELS]
        tiles.append(ref[...])
        msg_a[2 * plane : 2 * plane + 2, :] = ref[pl.ds(6 * even, 2), :]
        msg_b[2 * plane : 2 * plane + 2, :] = ref[pl.ds(6 - 6 * even, 2), :]
    for plane in range(OLD):
        ref = old.at[plane // LEVELS, plane % LEVELS]
        tiles.append(ref[...])
        at = 2 * PLANES + plane
        msg_a[at : at + 1, :] = ref[pl.ds(7 * even, 1), :]
        msg_b[at : at + 1, :] = ref[pl.ds(7 - 7 * even, 1), :]
    edges[...] = packed_edges(tiles)


def hold_kernel(off_hbm, frac_hbm, _, off, frac, sems):
    copies = [
        pltpu.make_async_copy(off_hbm, off, sems.at[0]),
        pltpu.make_async_copy(frac_hbm, frac, sems.at[1]),
    ]
    for copy in copies:
        copy.start()
    for copy in copies:
        copy.wait()


def rows_kernel(got_a, got_b, own_edges, outer, edges):
    even = lax.axis_index("gy") % 2 == 0
    above = jnp.where(even, got_a[...], got_b[...])
    below = jnp.where(even, got_b[...], got_a[...])
    outer[...] = jnp.zeros_like(outer)
    for plane in range(PLANES):
        outer[plane, 0:2, :] = above[2 * plane : 2 * plane + 2]
        outer[plane, 6:8, :] = below[2 * plane : 2 * plane + 2]
    for plane in range(PLANES, PLANES + OLD):
        outer[plane, 0:1, :] = above[PLANES + plane : PLANES + plane + 1]
        outer[plane, 7:8, :] = below[PLANES + plane : PLANES + plane + 1]
    edges[0:ROWS, :] = own_edges[...]
    edges[ROWS:, :] = packed_edges([outer[plane] for plane in range(PLANES + OLD)])


class Shifts:
    def __init__(self):
        shape = (LEVELS, ROWS, COLS)
        lane = lax.broadcasted_iota(jnp.int32, shape, 2)
        row = lax.broadcasted_iota(jnp.int32, shape, 1)
        self.lane_first, self.lane_last = lane == 0, lane == COLS - 1
        self.row_first, self.row_last = row == 0, row == ROWS - 1

    def east(self, here, other):
        return pltpu.roll(jnp.where(self.lane_first, other, here), COLS - 1, 2)

    def west(self, here, other):
        return pltpu.roll(jnp.where(self.lane_last, other, here), 1, 2)

    def north(self, here, other):
        return pltpu.roll(jnp.where(self.row_first, other, here), ROWS - 1, 1)

    def south(self, here, other):
        return pltpu.roll(jnp.where(self.row_last, other, here), 1, 1)


def weighted(low, mid, high):
    return 0.25 * low + 0.5 * mid + 0.25 * high


def vertical_slope(field):
    inner = (field[2:] - field[:-2]) * (0.5 / spacing_z)
    bottom = (field[1:2] - field[0:1]) * (1.0 / spacing_z)
    top = (field[-1:] - field[-2:-1]) * (1.0 / spacing_z)
    return jnp.concatenate([bottom, inner, top], axis=0)


def strain_parts(gradient):
    parts = [
        gradient[a][a] if a == b else 0.5 * (gradient[b][a] + gradient[a][b])
        for a, b in zip(PAIR_FIRST, PAIR_SECOND)
    ]
    total = parts[0] * parts[0] + parts[1] * parts[1] + parts[2] * parts[2]
    cross = parts[3] * parts[3] + parts[4] * parts[4] + parts[5] * parts[5]
    return parts, jnp.sqrt(2.0 * (total + 2.0 * cross))


def main_kernel(
    vel, old_lm, old_mm, offsets, fractions, outer, from_right, from_left, new_lm, new_mm, coefficient
):
    sh = Shifts()
    right = right_mask()
    halves = []
    for half in range(2):
        at = slice(half * ROWS, (half + 1) * ROWS)
        halves.append(jnp.where(right, from_right[at, :], from_left[at, :]))

    def four(first_plane, own):
        side = [
            jnp.stack(
                [
                    pltpu.roll(half, (COLS - edge_shift(first_plane + z)) % COLS, 1)
                    for z in range(LEVELS)
                ]
            )
            for half in halves
        ]
        return own, side[0], outer[first_plane : first_plane + LEVELS], side[1]

    fields = [four(LEVELS * c, vel[c]) for c in range(3)]
    west, east, along = [], [], []
    for tiles in fields:
        own, side, rows, corner = tiles
        west.append([sh.west(own, side), sh.west(side, own), sh.west(rows, corner), sh.west(corner, rows)])
        east.append([sh.east(own, side), sh.east(side, own), sh.east(rows, corner), sh.east(corner, rows)])
        along.append([weighted(west[-1][t], tiles[t], east[-1][t]) for t in range(4)])
    filtered = []
    for c in range(3):
        filtered.append(
            [
                weighted(sh.south(along[c][t], along[c][t ^ 2]), along[c][t], sh.north(along[c][t], along[c][t ^ 2]))
                for t in range(4)
            ]
        )
    modelled = []
    for t in range(4):
        gradient = [
            (
                0.5 * (east[c][t] - west[c][t]),
                0.5 * (sh.north(fields[c][t], fields[c][t ^ 2]) - sh.south(fields[c][t], fields[c][t ^ 2])),
                vertical_slope(fields[c][t]),
            )
            for c in range(3)
        ]
        parts, magnitude = strain_parts(gradient)
        modelled.append([magnitude * part for part in parts])
    own = [filtered[c][0] for c in range(3)]
    gradient = []
    for c in range(3):
        f, side, rows, _ = filtered[c]
        gradient.append(
            (
                0.5 * (sh.east(f, side) - sh.west(f, side)),
                0.5 * (sh.north(f, rows) - sh.south(f, rows)),
                vertical_slope(f),
            )
        )
    parts_f, magnitude_f = strain_parts(gradient)
    lm = mm = 0.0
    for pair, (a, b) in enumerate(zip(PAIR_FIRST, PAIR_SECOND)):
        line, model = [], []
        for t in (0, 2):
            line.append(
                weighted(west[a][t] * west[b][t], fields[a][t] * fields[b][t], east[a][t] * east[b][t])
            )
            here, side = modelled[t][pair], modelled[t + 1][pair]
            model.append(weighted(sh.west(here, side), here, sh.east(here, side)))
        product = weighted(sh.south(*line), line[0], sh.north(*line))
        smooth = weighted(sh.south(*model), model[0], sh.north(*model))
        resolved = product - own[a] * own[b]
        m = 2.0 * filter_area * (smooth - 4.0 * magnitude_f * parts_f[pair])
        weight = 1.0 if a == b else 2.0
        lm = lm + weight * resolved * m
        mm = mm + weight * m * m

    upstream = offsets[0] == 1
    f0, f1, f2 = fractions[0], fractions[1], fractions[2]
    back = offsets[1] == -1
    g0, g1, g2 = 1.0 - f0, 1.0 - f1, 1.0 - f2
    wx = (jnp.where(upstream, g0, 0.0), jnp.where(upstream, f0, g0), jnp.where(upstream, 0.0, f0))
    wy = (jnp.where(back, g1, 0.0), jnp.where(back, f1, g1), jnp.where(back, 0.0, f1))
    level = offsets[2]
    carried = []
    for k, ref in enumerate((old_lm, old_mm)):
        here, side, rows, corner = four(PLANES + LEVELS * k, ref[...])
        columns = [
            (sh.west(here, side), sh.west(rows, corner)),
            (here, rows),
            (sh.east(here, side), sh.east(rows, corner)),
        ]
        nine = [[sh.south(*pair), pair[0], sh.north(*pair)] for pair in columns]
        total = []
        for z in range(LEVELS):
            value = 0.0
            for s in range(max(z - 1, 0), min(z + 2, LEVELS)):
                weight = jnp.where(level[z] == s, g2[z], jnp.where(level[z] == s - 1, f2[z], 0.0))
                plane = 0.0
                for y in range(3):
                    row = wx[0][z] * nine[0][y][s] + wx[1][z] * nine[1][y][s] + wx[2][z] * nine[2][y][s]
                    plane = plane + wy[y][z] * row
                value = value + weight * plane
            total.append(value)
        carried.append(jnp.stack(total))
    lm_out = relax_rate * lm + (1.0 - relax_rate) * carried[0]
    mm_out = relax_rate * mm + (1.0 - relax_rate) * carried[1]
    new_lm[...] = lm_out
    new_mm[...] = mm_out
    coefficient[...] = jnp.maximum(lm_out, 0.0) / mm_out


def f32(*shape):
    return jax.ShapeDtypeStruct(shape, jnp.float32)


def kernel_call(kernel, outs, args, space=VMEM, scratch=(), limit=16 * 1024):
    return pl.pallas_call(
        kernel,
        out_shape=outs,
        in_specs=[space] * len(args) if isinstance(space, pl.BlockSpec) else space,
        out_specs=[VMEM] * len(outs),
        scratch_shapes=scratch,
        compiler_params=pltpu.CompilerParams(vmem_limit_bytes=limit * 1024),
    )(*args)


def even_pairs(count):
    return [(i, i ^ 1) for i in range(count)]


def odd_pairs(count):
    return [(i, (((i + 1) % count ^ 1) - 1) % count) for i in range(count)]


def body(velocity, old_lm, old_mm, offsets, fractions):
    nx, ny = lax.axis_size("gx"), lax.axis_size("gy")
    rows = 2 * PLANES + OLD
    msg_a, msg_b, own_edges = kernel_call(
        pack_kernel,
        [f32(rows, COLS), f32(rows, COLS), f32(ROWS, COLS)],
        (velocity, old_lm, old_mm),
        space=HBM,
        scratch=[
            pltpu.VMEM((3, LEVELS, ROWS, COLS), jnp.float32),
            pltpu.VMEM((2, LEVELS, ROWS, COLS), jnp.float32),
            pltpu.SemaphoreType.DMA((3,)),
        ],
        limit=55190,
    )
    got_a = lax.ppermute(msg_a, "gy", even_pairs(ny))
    got_b = lax.ppermute(msg_b, "gy", odd_pairs(ny))
    offsets, fractions = kernel_call(
        hold_kernel,
        [jax.ShapeDtypeStruct(offsets.shape, offsets.dtype), f32(3, LEVELS, ROWS, COLS)],
        (offsets, fractions, own_edges),
        space=[HBM, HBM, VMEM],
        scratch=[pltpu.SemaphoreType.DMA((2,))],
        limit=55116,
    )
    outer, edges = kernel_call(
        rows_kernel, [f32(PLANES + OLD, ROWS, COLS), f32(2 * ROWS, COLS)], (got_a, got_b, own_edges)
    )
    from_left = lax.ppermute(edges, "gx", [(i, (i + 1) % nx) for i in range(nx)])
    from_right = lax.ppermute(edges, "gx", [((i + 1) % nx, i) for i in range(nx)])
    out = f32(LEVELS, ROWS, COLS)
    return tuple(
        kernel_call(
            main_kernel,
            [out, out, out],
            (velocity, old_lm, old_mm, offsets, fractions, outer, from_right, from_left),
        )
    )


def solution(mesh):
    placed = (
        P(None, None, "gy", "gx"),
        P(None, "gy", "gx"),
        P(None, "gy", "gx"),
        P(None, None, "gy", "gx"),
        P(None, None, "gy", "gx"),
    )
    return jax.shard_map(
        body,
        mesh=mesh,
        in_specs=placed,
        out_specs=(P(None, "gy", "gx"), P(None, "gy", "gx"), P(None, "gy", "gx")),
        check_vma=False,
    )
```

```python
import jax
import jax.numpy as jnp
from jax import lax
from jax.experimental import pallas as pl
from jax.experimental.pallas import tpu as pltpu
from jax.sharding import PartitionSpec as P

relax_rate = 0.3
filter_area = 0.63
spacing_z = 0.5
PAIR_FIRST = (0, 1, 2, 0, 0, 1)
PAIR_SECOND = (0, 1, 2, 1, 2, 2)
LEVELS = 4
ROWS = 8
COLS = 128
FIELDS = 5
PLANES = 3 * LEVELS
OLD = 2 * LEVELS
GROUP = 16
VMEM = pl.BlockSpec(memory_space=pltpu.VMEM)
HBM = pl.BlockSpec(memory_space=pltpu.HBM)


def lanes():
    return lax.broadcasted_iota(jnp.int32, (ROWS, COLS), 1)


def packed_edges(tile):
    lane = lanes()
    packed = None
    for z in range(LEVELS):
        for field in range(FIELDS):
            first = GROUP * z + (4 * field if field < 3 else 12 + 2 * (field - 3))
            moved = pltpu.roll(tile(field, z), first + (2 if field < 3 else 1), 1)
            packed = moved if packed is None else jnp.where(lane >= first, moved, packed)
    return packed


def from_right_mask():
    lane = lanes() % GROUP
    return jnp.where(lane < 12, lane % 4, 2 * (lane % 2)) >= 2


def edge_domain(tile):
    lane = lanes()
    inner = lane % GROUP < 6
    packed = None
    for z in range(LEVELS):
        at = GROUP * z
        plane = tile(z)
        moved = jnp.where(inner, pltpu.roll(plane, at + 4, 1), pltpu.roll(plane, at + 8, 1))
        packed = moved if packed is None else jnp.where(lane >= at, moved, packed)
    return packed


def pack_kernel(vel_hbm, lm_hbm, mm_hbm, msg_a, msg_b, vel, old, sems):
    pairs = ((vel_hbm, vel), (lm_hbm, old.at[0]), (mm_hbm, old.at[1]))
    copies = [pltpu.make_async_copy(*pair, sems.at[k]) for k, pair in enumerate(pairs)]
    for copy in copies:
        copy.start()
    even = 1 - lax.axis_index("gy") % 2
    for copy in copies:
        copy.wait()
    for plane in range(PLANES):
        ref = vel.at[plane // LEVELS, plane % LEVELS]
        msg_a[2 * plane : 2 * plane + 2, :] = ref[pl.ds(6 * even, 2), :]
        msg_b[2 * plane : 2 * plane + 2, :] = ref[pl.ds(6 - 6 * even, 2), :]
    for plane in range(OLD):
        ref = old.at[plane // LEVELS, plane % LEVELS]
        at = 2 * PLANES + plane
        msg_a[at : at + 1, :] = ref[pl.ds(7 * even, 1), :]
        msg_b[at : at + 1, :] = ref[pl.ds(7 - 7 * even, 1), :]


def hold_kernel(
    off_hbm, frac_hbm, vel_hbm, lm_hbm, mm_hbm, _,
    off, frac, edges, near, near_off, near_frac, vel, old, sems,
):
    pairs = (
        (vel_hbm, vel), (lm_hbm, old.at[0]), (mm_hbm, old.at[1]), (off_hbm, off), (frac_hbm, frac)
    )
    copies = [pltpu.make_async_copy(*pair, sems.at[k]) for k, pair in enumerate(pairs)]
    for copy in copies:
        copy.start()
    for copy in copies:
        copy.wait()

    def tile(field, z):
        return vel[field, z] if field < 3 else old[field - 3, z]

    edges[...] = packed_edges(tile)
    for field in range(FIELDS):
        near[field] = edge_domain(lambda z: tile(field, z))
    for k in range(3):
        near_off[k] = edge_domain(lambda z: off[k, z])
        near_frac[k] = edge_domain(lambda z: frac[k, z])


def rows_kernel(got_a, got_b, own_edges, outer, edges):
    even = lax.axis_index("gy") % 2 == 0
    above = jnp.where(even, got_a[...], got_b[...])
    below = jnp.where(even, got_b[...], got_a[...])
    outer[...] = jnp.zeros_like(outer)
    for plane in range(PLANES):
        outer[plane, 0:2, :] = above[2 * plane : 2 * plane + 2]
        outer[plane, 6:8, :] = below[2 * plane : 2 * plane + 2]
    for plane in range(PLANES, PLANES + OLD):
        outer[plane, 0:1, :] = above[PLANES + plane : PLANES + plane + 1]
        outer[plane, 7:8, :] = below[PLANES + plane : PLANES + plane + 1]
    edges[0:ROWS, :] = own_edges[...]
    edges[ROWS:, :] = packed_edges(lambda field, z: outer[LEVELS * field + z])


class Grid:
    def __init__(self, shape=(LEVELS, ROWS, COLS)):
        self.rows = len(shape) - 2
        row = lax.broadcasted_iota(jnp.int32, shape, self.rows)
        self.row_first, self.row_last = row == 0, row == ROWS - 1
        self.level = self.levels(shape)

    def levels(self, shape):
        return lax.broadcasted_iota(jnp.int32, shape, 0)

    def east(self, tile):
        return pltpu.roll(tile, COLS - 1, self.rows + 1)

    def west(self, tile):
        return pltpu.roll(tile, 1, self.rows + 1)

    def north(self, here, other):
        return pltpu.roll(jnp.where(self.row_first, other, here), ROWS - 1, self.rows)

    def south(self, here, other):
        return pltpu.roll(jnp.where(self.row_last, other, here), 1, self.rows)

    def twice_slope(self, field):
        inner = (field[2:] - field[:-2]) * (1.0 / spacing_z)
        bottom = (field[1:2] - field[0:1]) * (2.0 / spacing_z)
        top = (field[-1:] - field[-2:-1]) * (2.0 / spacing_z)
        return jnp.concatenate([bottom, inner, top], axis=0)

    def nine(self, own, rows):
        three = (self.south(own, rows), own, self.north(own, rows))
        return [(self.west(t), t, self.east(t)) for t in three]

    def by_level(self, own, rows):
        here = self.nine(own, rows)
        down = [[jnp.concatenate([t[:1], t[:-1]], axis=0) for t in row] for row in here]
        up = [[jnp.concatenate([t[1:], t[-1:]], axis=0) for t in row] for row in here]
        return down, here, up


class EdgeGrid(Grid):
    def __init__(self):
        super().__init__((ROWS, COLS))

    def levels(self, shape):
        return lanes() // GROUP

    def above(self, tile):
        return pltpu.roll(tile, COLS - GROUP, 1)

    def below(self, tile):
        return pltpu.roll(tile, GROUP, 1)

    def twice_slope(self, field):
        bottom, top = self.level == 0, self.level == LEVELS - 1
        high = jnp.where(top, field, self.above(field))
        low = jnp.where(bottom, field, self.below(field))
        return (high - low) * jnp.where(bottom | top, 2.0 / spacing_z, 1.0 / spacing_z)

    def by_level(self, own, rows):
        return (
            self.nine(self.below(own), self.below(rows)),
            self.nine(own, rows),
            self.nine(self.above(own), self.above(rows)),
        )


def spread(low, mid, high):
    return (low + high) + (mid + mid)


def strains(gradient):
    parts = [
        gradient[a][a] if a == b else gradient[b][a] + gradient[a][b]
        for a, b in zip(PAIR_FIRST, PAIR_SECOND)
    ]
    diagonal = parts[0] * parts[0] + parts[1] * parts[1] + parts[2] * parts[2]
    cross = parts[3] * parts[3] + parts[4] * parts[4] + parts[5] * parts[5]
    return parts, jnp.sqrt((diagonal + diagonal) + cross)


def update(grid, fields, offsets, fractions):
    filtered, gradients = [], []
    for own, rows in fields[:3]:
        tiles = (own, rows)
        west = [grid.west(t) for t in tiles]
        east = [grid.east(t) for t in tiles]
        along = [spread(west[t], tiles[t], east[t]) for t in range(2)]
        filtered.append(
            [
                spread(grid.south(along[t], along[1 - t]), along[t], grid.north(along[t], along[1 - t]))
                for t in range(2)
            ]
        )
        gradients.append(
            [
                (
                    east[t] - west[t],
                    grid.north(tiles[t], tiles[1 - t]) - grid.south(tiles[t], tiles[1 - t]),
                    grid.twice_slope(tiles[t]),
                )
                for t in range(2)
            ]
        )
    modelled = []
    for t in range(2):
        parts, magnitude = strains([gradients[c][t] for c in range(3)])
        modelled.append([magnitude * part for part in parts])
    own_f = [filtered[c][0] for c in range(3)]
    parts_f, magnitude_f = strains(
        [
            (
                grid.east(f) - grid.west(f),
                grid.north(f, rows) - grid.south(f, rows),
                grid.twice_slope(f),
            )
            for f, rows in filtered
        ]
    )

    def both_ways(own, rows):
        t = spread(grid.south(own, rows), own, grid.north(own, rows))
        return spread(grid.west(t), t, grid.east(t))

    product_sum = diagonal = cross = 0.0
    for pair, (a, b) in enumerate(zip(PAIR_FIRST, PAIR_SECOND)):
        product = both_ways(fields[a][0] * fields[b][0], fields[a][1] * fields[b][1])
        resolved = 16.0 * product - own_f[a] * own_f[b]
        smooth = both_ways(modelled[0][pair], modelled[1][pair])
        m = 4.0 * smooth - magnitude_f * parts_f[pair]
        product_sum = product_sum + resolved * m
        if a == b:
            diagonal = diagonal + m * m
        else:
            cross = cross + m * m
    scale = 2.0 * filter_area / 256.0
    lm = product_sum * (scale / 256.0)
    mm = (diagonal + 0.5 * cross) * (scale * scale)

    upstream = offsets[0] == 1
    back = offsets[1] == -1
    at_level, one_below = offsets[2] == grid.level, offsets[2] == grid.level - 1
    f0, f1, f2 = fractions
    g0, g1, g2 = 1.0 - f0, 1.0 - f1, 1.0 - f2
    wx = (jnp.where(upstream, g0, 0.0), jnp.where(upstream, f0, g0), jnp.where(upstream, 0.0, f0))
    wy = (jnp.where(back, g1, 0.0), jnp.where(back, f1, g1), jnp.where(back, 0.0, f1))
    wz = (
        jnp.where(one_below, g2, 0.0),
        jnp.where(at_level, g2, jnp.where(one_below, f2, 0.0)),
        jnp.where(at_level, f2, 0.0),
    )
    results = []
    for germano, (own, rows) in ((lm, fields[3]), (mm, fields[4])):
        carried = 0.0
        for weight, nine in zip(wz, grid.by_level(own, rows)):
            plane = 0.0
            for y in range(3):
                plane = plane + wy[y] * (wx[0] * nine[y][0] + wx[1] * nine[y][1] + wx[2] * nine[y][2])
            carried = carried + weight * plane
        results.append(relax_rate * germano + (1.0 - relax_rate) * carried)
    return results


def inner_kernel(vel, old_lm, old_mm, offsets, fractions, outer, new, near_rows):
    fields = [vel[c] for c in range(3)] + [old_lm[...], old_mm[...]]
    fields = [(own, outer[LEVELS * f : LEVELS * (f + 1)]) for f, own in enumerate(fields)]
    new[0], new[1] = update(Grid(), fields, [offsets[k] for k in range(3)], [fractions[k] for k in range(3)])
    for field in range(FIELDS):
        near_rows[field] = edge_domain(lambda z: outer[LEVELS * field + z])


def edge_kernel(
    inner, near, near_rows, near_off, near_frac, from_right, from_left, new_lm, new_mm, coefficient
):
    right = from_right_mask()
    place = lanes() % GROUP
    is_right, is_left = (place == 4) | (place == 5), (place == 6) | (place == 7)
    pairs = [[], []]
    for half, own in enumerate((near, near_rows)):
        at = slice(half * ROWS, (half + 1) * ROWS)
        halo = jnp.where(right, from_right[at, :], from_left[at, :])
        for field in range(FIELDS):
            first = 4 * field if field < 3 else 12 + 2 * (field - 3)
            to_right = (4 - first - (2 if field < 3 else 1)) % COLS
            to_left = ((6 if field < 3 else 7) - first) % COLS
            tile = jnp.where(is_left, pltpu.roll(halo, to_left, 1), own[field])
            pairs[half].append(jnp.where(is_right, pltpu.roll(halo, to_right, 1), tile))
    fields = list(zip(*pairs))
    edge = update(EdgeGrid(), fields, [near_off[k] for k in range(3)], [near_frac[k] for k in range(3)])
    lane = lanes()
    for z in range(LEVELS):
        out = []
        for k in range(2):
            low = pltpu.roll(edge[k], (COLS - GROUP * z - 8) % COLS, 1)
            high = pltpu.roll(edge[k], (COLS - 4 - GROUP * z) % COLS, 1)
            out.append(jnp.where(lane < 2, low, jnp.where(lane >= COLS - 2, high, inner[k, z])))
        new_lm[z] = out[0]
        new_mm[z] = out[1]
        coefficient[z] = jnp.maximum(out[0], 0.0) / out[1]


def f32(*shape):
    return jax.ShapeDtypeStruct(shape, jnp.float32)


def i32(*shape):
    return jax.ShapeDtypeStruct(shape, jnp.int32)


def kernel_call(kernel, outs, args, spaces=None, scratch=(), limit=16 * 1024):
    return pl.pallas_call(
        kernel,
        out_shape=outs,
        in_specs=[VMEM] * len(args) if spaces is None else spaces,
        out_specs=[VMEM] * len(outs),
        scratch_shapes=scratch,
        compiler_params=pltpu.CompilerParams(vmem_limit_bytes=limit * 1024),
    )(*args)


def even_pairs(count):
    return [(i, i ^ 1) for i in range(count)]


def odd_pairs(count):
    return [(i, (((i + 1) % count ^ 1) - 1) % count) for i in range(count)]


def body(velocity, old_lm, old_mm, offsets, fractions):
    nx, ny = lax.axis_size("gx"), lax.axis_size("gy")
    rows = 2 * PLANES + OLD
    held = [
        pltpu.VMEM((3, LEVELS, ROWS, COLS), jnp.float32),
        pltpu.VMEM((2, LEVELS, ROWS, COLS), jnp.float32),
    ]
    msg_a, msg_b = kernel_call(
        pack_kernel,
        [f32(rows, COLS), f32(rows, COLS)],
        (velocity, old_lm, old_mm),
        spaces=[HBM] * 3,
        scratch=held + [pltpu.SemaphoreType.DMA((3,))],
        limit=55190,
    )
    got_a = lax.ppermute(msg_a, "gy", even_pairs(ny))
    got_b = lax.ppermute(msg_b, "gy", odd_pairs(ny))
    tile = (ROWS, COLS)
    offsets, fractions, own_edges, near, near_off, near_frac = kernel_call(
        hold_kernel,
        [
            i32(3, LEVELS, *tile), f32(3, LEVELS, *tile), f32(*tile),
            f32(FIELDS, *tile), i32(3, *tile), f32(3, *tile),
        ],
        (offsets, fractions, velocity, old_lm, old_mm, msg_b),
        spaces=[HBM] * 5 + [VMEM],
        scratch=held + [pltpu.SemaphoreType.DMA((5,))],
        limit=55030,
    )
    outer, edges = kernel_call(
        rows_kernel, [f32(PLANES + OLD, *tile), f32(2 * ROWS, COLS)], (got_a, got_b, own_edges)
    )
    from_left = lax.ppermute(edges, "gx", [(i, (i + 1) % nx) for i in range(nx)])
    from_right = lax.ppermute(edges, "gx", [((i + 1) % nx, i) for i in range(nx)])
    inner, near_rows = kernel_call(
        inner_kernel,
        [f32(2, LEVELS, *tile), f32(FIELDS, *tile)],
        (velocity, old_lm, old_mm, offsets, fractions, outer),
    )
    out = f32(LEVELS, *tile)
    return tuple(
        kernel_call(
            edge_kernel,
            [out, out, out],
            (inner, near, near_rows, near_off, near_frac, from_right, from_left),
        )
    )


def solution(mesh):
    placed = (
        P(None, None, "gy", "gx"),
        P(None, "gy", "gx"),
        P(None, "gy", "gx"),
        P(None, None, "gy", "gx"),
        P(None, None, "gy", "gx"),
    )
    return jax.shard_map(
        body,
        mesh=mesh,
        in_specs=placed,
        out_specs=(P(None, "gy", "gx"), P(None, "gy", "gx"), P(None, "gy", "gx")),
        check_vma=False,
    )
```

```python
import jax
import jax.numpy as jnp
from jax import lax
from jax.experimental import pallas as pl
from jax.experimental.pallas import tpu as pltpu
from jax.sharding import PartitionSpec as P

relax_rate = 0.3
filter_area = 0.63
spacing_z = 0.5
PAIR_FIRST = (0, 1, 2, 0, 0, 1)
PAIR_SECOND = (0, 1, 2, 1, 2, 2)
LEVELS = 4
ROWS = 8
COLS = 128
FIELDS = 5
PLANES = 3 * LEVELS
OLD = 2 * LEVELS
GROUP = 16
VMEM = pl.BlockSpec(memory_space=pltpu.VMEM)
HBM = pl.BlockSpec(memory_space=pltpu.HBM)


def lanes():
    return lax.broadcasted_iota(jnp.int32, (ROWS, COLS), 1)


def packed_edges(tile):
    lane = lanes()
    packed = None
    for z in range(LEVELS):
        for field in range(FIELDS):
            first = GROUP * z + (4 * field if field < 3 else 12 + 2 * (field - 3))
            moved = pltpu.roll(tile(field, z), first + (2 if field < 3 else 1), 1)
            packed = moved if packed is None else jnp.where(lane >= first, moved, packed)
    return packed


def from_right_mask():
    lane = lanes() % GROUP
    return jnp.where(lane < 12, lane % 4, 2 * (lane % 2)) >= 2


def edge_domain(tile):
    lane = lanes()
    inner = lane % GROUP < 6
    packed = None
    for z in range(LEVELS):
        at = GROUP * z
        plane = tile(z)
        moved = jnp.where(inner, pltpu.roll(plane, at + 4, 1), pltpu.roll(plane, at + 8, 1))
        packed = moved if packed is None else jnp.where(lane >= at, moved, packed)
    return packed


def pack_kernel(vel_hbm, lm_hbm, mm_hbm, msg_a, msg_b, vel, old, sems):
    pairs = ((vel_hbm, vel), (lm_hbm, old.at[0]), (mm_hbm, old.at[1]))
    copies = [pltpu.make_async_copy(*pair, sems.at[k]) for k, pair in enumerate(pairs)]
    for copy in copies:
        copy.start()
    even = 1 - lax.axis_index("gy") % 2
    for copy in copies:
        copy.wait()
    for plane in range(PLANES):
        ref = vel.at[plane // LEVELS, plane % LEVELS]
        msg_a[2 * plane : 2 * plane + 2, :] = ref[pl.ds(6 * even, 2), :]
        msg_b[2 * plane : 2 * plane + 2, :] = ref[pl.ds(6 - 6 * even, 2), :]
    for plane in range(OLD):
        ref = old.at[plane // LEVELS, plane % LEVELS]
        at = 2 * PLANES + plane
        msg_a[at : at + 1, :] = ref[pl.ds(7 * even, 1), :]
        msg_b[at : at + 1, :] = ref[pl.ds(7 - 7 * even, 1), :]


def fill_outer(above, below, outer):
    outer[...] = jnp.zeros_like(outer)
    for plane in range(PLANES):
        outer[plane, 0:2, :] = above[2 * plane : 2 * plane + 2]
        outer[plane, 6:8, :] = below[2 * plane : 2 * plane + 2]
    for plane in range(PLANES, PLANES + OLD):
        outer[plane, 0:1, :] = above[PLANES + plane : PLANES + plane + 1]
        outer[plane, 7:8, :] = below[PLANES + plane : PLANES + plane + 1]


def first_edges_kernel(got_a, vel, old_lm, old_mm, own_edges, edges, wide, outer):
    def tile(field, z):
        return vel[field, z] if field < 3 else (old_lm, old_mm)[field - 3][z]

    own_edges[...] = packed_edges(tile)
    wide[0:ROWS, :] = own_edges[...]
    wide[ROWS:, :] = jnp.zeros_like(wide[ROWS:, :])
    fill_outer(got_a[...], got_a[...], outer)
    edges[0:ROWS, :] = own_edges[...]
    edges[ROWS:, :] = packed_edges(lambda field, z: outer[LEVELS * field + z])


def rows_kernel(got_a, got_b, own_edges, outer, edges):
    even = lax.axis_index("gy") % 2 == 0
    above = jnp.where(even, got_a[...], got_b[...])
    below = jnp.where(even, got_b[...], got_a[...])
    fill_outer(above, below, outer)
    edges[0:ROWS, :] = own_edges[...]
    edges[ROWS:, :] = packed_edges(lambda field, z: outer[LEVELS * field + z])


class Grid:
    def __init__(self, shape=(LEVELS, ROWS, COLS)):
        self.rows = len(shape) - 2
        row = lax.broadcasted_iota(jnp.int32, shape, self.rows)
        self.row_first, self.row_last = row == 0, row == ROWS - 1
        self.level = self.levels(shape)

    def levels(self, shape):
        return lax.broadcasted_iota(jnp.int32, shape, 0)

    def east(self, tile):
        return pltpu.roll(tile, COLS - 1, self.rows + 1)

    def west(self, tile):
        return pltpu.roll(tile, 1, self.rows + 1)

    def north(self, here, other):
        return pltpu.roll(jnp.where(self.row_first, other, here), ROWS - 1, self.rows)

    def south(self, here, other):
        return pltpu.roll(jnp.where(self.row_last, other, here), 1, self.rows)

    def twice_slope(self, field):
        inner = (field[2:] - field[:-2]) * (1.0 / spacing_z)
        bottom = (field[1:2] - field[0:1]) * (2.0 / spacing_z)
        top = (field[-1:] - field[-2:-1]) * (2.0 / spacing_z)
        return jnp.concatenate([bottom, inner, top], axis=0)

    def nine(self, own, rows):
        three = (self.south(own, rows), own, self.north(own, rows))
        return [(self.west(t), t, self.east(t)) for t in three]

    def by_level(self, own, rows):
        here = self.nine(own, rows)
        down = [[jnp.concatenate([t[:1], t[:-1]], axis=0) for t in row] for row in here]
        up = [[jnp.concatenate([t[1:], t[-1:]], axis=0) for t in row] for row in here]
        return down, here, up


class EdgeGrid(Grid):
    def __init__(self):
        super().__init__((ROWS, COLS))

    def levels(self, shape):
        return lanes() // GROUP

    def above(self, tile):
        return pltpu.roll(tile, COLS - GROUP, 1)

    def below(self, tile):
        return pltpu.roll(tile, GROUP, 1)

    def twice_slope(self, field):
        bottom, top = self.level == 0, self.level == LEVELS - 1
        high = jnp.where(top, field, self.above(field))
        low = jnp.where(bottom, field, self.below(field))
        return (high - low) * jnp.where(bottom | top, 2.0 / spacing_z, 1.0 / spacing_z)

    def by_level(self, own, rows):
        return (
            self.nine(self.below(own), self.below(rows)),
            self.nine(own, rows),
            self.nine(self.above(own), self.above(rows)),
        )


def spread(low, mid, high):
    return (low + high) + (mid + mid)


def strains(gradient):
    parts = [
        gradient[a][a] if a == b else gradient[b][a] + gradient[a][b]
        for a, b in zip(PAIR_FIRST, PAIR_SECOND)
    ]
    diagonal = parts[0] * parts[0] + parts[1] * parts[1] + parts[2] * parts[2]
    cross = parts[3] * parts[3] + parts[4] * parts[4] + parts[5] * parts[5]
    return parts, jnp.sqrt((diagonal + diagonal) + cross)


def update(grid, fields, offsets, fractions):
    filtered, gradients = [], []
    for own, rows in fields[:3]:
        tiles = (own, rows)
        west = [grid.west(t) for t in tiles]
        east = [grid.east(t) for t in tiles]
        along = [spread(west[t], tiles[t], east[t]) for t in range(2)]
        filtered.append(
            [
                spread(grid.south(along[t], along[1 - t]), along[t], grid.north(along[t], along[1 - t]))
                for t in range(2)
            ]
        )
        gradients.append(
            [
                (
                    east[t] - west[t],
                    grid.north(tiles[t], tiles[1 - t]) - grid.south(tiles[t], tiles[1 - t]),
                    grid.twice_slope(tiles[t]),
                )
                for t in range(2)
            ]
        )
    modelled = []
    for t in range(2):
        parts, magnitude = strains([gradients[c][t] for c in range(3)])
        modelled.append([magnitude * part for part in parts])
    own_f = [filtered[c][0] for c in range(3)]
    parts_f, magnitude_f = strains(
        [
            (
                grid.east(f) - grid.west(f),
                grid.north(f, rows) - grid.south(f, rows),
                grid.twice_slope(f),
            )
            for f, rows in filtered
        ]
    )

    def both_ways(own, rows):
        t = spread(grid.south(own, rows), own, grid.north(own, rows))
        return spread(grid.west(t), t, grid.east(t))

    product_sum = diagonal = cross = 0.0
    for pair, (a, b) in enumerate(zip(PAIR_FIRST, PAIR_SECOND)):
        product = both_ways(fields[a][0] * fields[b][0], fields[a][1] * fields[b][1])
        resolved = 16.0 * product - own_f[a] * own_f[b]
        smooth = both_ways(modelled[0][pair], modelled[1][pair])
        m = 4.0 * smooth - magnitude_f * parts_f[pair]
        product_sum = product_sum + resolved * m
        if a == b:
            diagonal = diagonal + m * m
        else:
            cross = cross + m * m
    scale = 2.0 * filter_area / 256.0
    lm = product_sum * (scale / 256.0)
    mm = (diagonal + 0.5 * cross) * (scale * scale)

    upstream = offsets[0] == 1
    back = offsets[1] == -1
    at_level, one_below = offsets[2] == grid.level, offsets[2] == grid.level - 1
    f0, f1, f2 = fractions
    g0, g1, g2 = 1.0 - f0, 1.0 - f1, 1.0 - f2
    wx = (jnp.where(upstream, g0, 0.0), jnp.where(upstream, f0, g0), jnp.where(upstream, 0.0, f0))
    wy = (jnp.where(back, g1, 0.0), jnp.where(back, f1, g1), jnp.where(back, 0.0, f1))
    wz = (
        jnp.where(one_below, g2, 0.0),
        jnp.where(at_level, g2, jnp.where(one_below, f2, 0.0)),
        jnp.where(at_level, f2, 0.0),
    )
    results = []
    for germano, (own, rows) in ((lm, fields[3]), (mm, fields[4])):
        carried = 0.0
        for weight, nine in zip(wz, grid.by_level(own, rows)):
            plane = 0.0
            for y in range(3):
                plane = plane + wy[y] * (wx[0] * nine[y][0] + wx[1] * nine[y][1] + wx[2] * nine[y][2])
            carried = carried + weight * plane
        results.append(relax_rate * germano + (1.0 - relax_rate) * carried)
    return results


def inner_kernel(
    vel, old_lm, old_mm, offsets, fractions, outer, new, near, near_rows, near_off, near_frac
):
    fields = [vel[c] for c in range(3)] + [old_lm[...], old_mm[...]]
    fields = [(own, outer[LEVELS * f : LEVELS * (f + 1)]) for f, own in enumerate(fields)]
    new[0], new[1] = update(Grid(), fields, [offsets[k] for k in range(3)], [fractions[k] for k in range(3)])
    for field, (own, rows) in enumerate(fields):
        near[field] = edge_domain(lambda z: own[z])
        near_rows[field] = edge_domain(lambda z: rows[z])
    for k in range(3):
        near_off[k] = edge_domain(lambda z: offsets[k, z])
        near_frac[k] = edge_domain(lambda z: fractions[k, z])


def edge_kernel(
    inner, near, near_rows, near_off, near_frac, from_right, left_a, left_b, new_lm, new_mm, coefficient
):
    right = from_right_mask()
    place = lanes() % GROUP
    is_right, is_left = (place == 4) | (place == 5), (place == 6) | (place == 7)
    even = lax.axis_index("gy") % 2 == 0
    upper = lax.broadcasted_iota(jnp.int32, (ROWS, COLS), 0) < ROWS // 2
    first, second = left_a[ROWS:, :], left_b[0:ROWS, :]
    corners = jnp.where(even, jnp.where(upper, first, second), jnp.where(upper, second, first))
    from_left = (left_a[0:ROWS, :], corners)
    pairs = [[], []]
    for half, own in enumerate((near, near_rows)):
        halo = jnp.where(right, from_right[half * ROWS : (half + 1) * ROWS, :], from_left[half])
        for field in range(FIELDS):
            first = 4 * field if field < 3 else 12 + 2 * (field - 3)
            to_right = (4 - first - (2 if field < 3 else 1)) % COLS
            to_left = ((6 if field < 3 else 7) - first) % COLS
            tile = jnp.where(is_left, pltpu.roll(halo, to_left, 1), own[field])
            pairs[half].append(jnp.where(is_right, pltpu.roll(halo, to_right, 1), tile))
    fields = list(zip(*pairs))
    edge = update(EdgeGrid(), fields, [near_off[k] for k in range(3)], [near_frac[k] for k in range(3)])
    lane = lanes()
    for z in range(LEVELS):
        out = []
        for k in range(2):
            low = pltpu.roll(edge[k], (COLS - GROUP * z - 8) % COLS, 1)
            high = pltpu.roll(edge[k], (COLS - 4 - GROUP * z) % COLS, 1)
            out.append(jnp.where(lane < 2, low, jnp.where(lane >= COLS - 2, high, inner[k, z])))
        new_lm[z] = out[0]
        new_mm[z] = out[1]
        coefficient[z] = jnp.maximum(out[0], 0.0) / out[1]


def f32(*shape):
    return jax.ShapeDtypeStruct(shape, jnp.float32)


def i32(*shape):
    return jax.ShapeDtypeStruct(shape, jnp.int32)


def kernel_call(kernel, outs, args, spaces=None, scratch=(), limit=16 * 1024):
    return pl.pallas_call(
        kernel,
        out_shape=outs,
        in_specs=[VMEM] * len(args) if spaces is None else spaces,
        out_specs=[VMEM] * len(outs),
        scratch_shapes=scratch,
        compiler_params=pltpu.CompilerParams(vmem_limit_bytes=limit * 1024),
    )(*args)


def even_pairs(count):
    return [(i, i ^ 1) for i in range(count)]


def odd_pairs(count):
    return [(i, (((i + 1) % count ^ 1) - 1) % count) for i in range(count)]


def body(velocity, old_lm, old_mm, offsets, fractions):
    nx, ny = lax.axis_size("gx"), lax.axis_size("gy")
    rows = 2 * PLANES + OLD
    held = [
        pltpu.VMEM((3, LEVELS, ROWS, COLS), jnp.float32),
        pltpu.VMEM((2, LEVELS, ROWS, COLS), jnp.float32),
    ]
    msg_a, msg_b = kernel_call(
        pack_kernel,
        [f32(rows, COLS), f32(rows, COLS)],
        (velocity, old_lm, old_mm),
        spaces=[HBM] * 3,
        scratch=held + [pltpu.SemaphoreType.DMA((3,))],
        limit=55190,
    )
    got_a = lax.ppermute(msg_a, "gy", even_pairs(ny))
    got_b = lax.ppermute(msg_b, "gy", odd_pairs(ny))
    tile = (ROWS, COLS)
    own_edges, edges, wide = kernel_call(
        first_edges_kernel,
        [f32(*tile), f32(2 * ROWS, COLS), f32(3 * ROWS, COLS)],
        (got_a, velocity, old_lm, old_mm),
        scratch=[pltpu.VMEM((PLANES + OLD, *tile), jnp.float32)],
    )
    to_east = [(i, (i + 1) % nx) for i in range(nx)]
    left_a = lax.ppermute(edges, "gx", to_east)
    left_b = lax.ppermute(
        wide, ("gx", "gy"), [(i * ny + j, k * ny + m) for i, k in to_east for j, m in odd_pairs(ny)]
    )
    outer, edges = kernel_call(
        rows_kernel, [f32(PLANES + OLD, *tile), f32(2 * ROWS, COLS)], (got_a, got_b, own_edges)
    )
    from_right = lax.ppermute(edges, "gx", [(k, i) for i, k in to_east])
    inner, near, near_rows, near_off, near_frac = kernel_call(
        inner_kernel,
        [f32(2, LEVELS, *tile), f32(FIELDS, *tile), f32(FIELDS, *tile), i32(3, *tile), f32(3, *tile)],
        (velocity, old_lm, old_mm, offsets, fractions, outer),
    )
    out = f32(LEVELS, *tile)
    return tuple(
        kernel_call(
            edge_kernel,
            [out, out, out],
            (inner, near, near_rows, near_off, near_frac, from_right, left_a, left_b),
        )
    )


def solution(mesh):
    placed = (
        P(None, None, "gy", "gx"),
        P(None, "gy", "gx"),
        P(None, "gy", "gx"),
        P(None, None, "gy", "gx"),
        P(None, None, "gy", "gx"),
    )
    return jax.shard_map(
        body,
        mesh=mesh,
        in_specs=placed,
        out_specs=(P(None, "gy", "gx"), P(None, "gy", "gx"), P(None, "gy", "gx")),
        check_vma=False,
    )
```

```python
import jax
import jax.numpy as jnp
from jax import lax
from jax.experimental import pallas as pl
from jax.experimental.pallas import tpu as pltpu
from jax.sharding import PartitionSpec as P

relax_rate = 0.3
filter_area = 0.63
spacing_z = 0.5
PAIR_FIRST = (0, 1, 2, 0, 0, 1)
PAIR_SECOND = (0, 1, 2, 1, 2, 2)
LEVELS = 4
ROWS = 8
COLS = 128
FIELDS = 5
PLANES = 3 * LEVELS
OLD = 2 * LEVELS
HALF = COLS // 2
GROUP = 16
VMEM = pl.BlockSpec(memory_space=pltpu.VMEM)
HBM = pl.BlockSpec(memory_space=pltpu.HBM)


def lanes():
    return lax.broadcasted_iota(jnp.int32, (ROWS, COLS), 1)


def packed_edges(tile, base=0):
    lane = lanes()
    packed = None
    for z in range(LEVELS):
        for field in range(FIELDS):
            first = base + GROUP * z + (4 * field if field < 3 else 12 + 2 * (field - 3))
            moved = pltpu.roll(tile(field, z), first + (2 if field < 3 else 1), 1)
            packed = moved if packed is None else jnp.where(lane >= first, moved, packed)
    return packed


def edge_domain(tile):
    lane = lanes()
    inner = lane % GROUP < 6
    packed = None
    for z in range(LEVELS):
        at = GROUP * z
        plane = tile(z)
        moved = jnp.where(inner, pltpu.roll(plane, at + 4, 1), pltpu.roll(plane, at + 8, 1))
        packed = moved if packed is None else jnp.where(lane >= at, moved, packed)
    return packed


def pack_kernel(vel_hbm, lm_hbm, mm_hbm, msg_a, msg_b, vel, old, sems):
    pairs = ((vel_hbm, vel), (lm_hbm, old.at[0]), (mm_hbm, old.at[1]))
    copies = [pltpu.make_async_copy(*pair, sems.at[k]) for k, pair in enumerate(pairs)]
    for copy in copies:
        copy.start()
    even = 1 - lax.axis_index("gy") % 2
    for copy in copies:
        copy.wait()
    for plane in range(PLANES):
        ref = vel.at[plane // LEVELS, plane % LEVELS]
        msg_a[2 * plane : 2 * plane + 2, :] = ref[pl.ds(6 * even, 2), :]
        msg_b[2 * plane : 2 * plane + 2, :] = ref[pl.ds(6 - 6 * even, 2), :]
    for plane in range(OLD):
        ref = old.at[plane // LEVELS, plane % LEVELS]
        at = 2 * PLANES + plane
        msg_a[at : at + 1, :] = ref[pl.ds(7 * even, 1), :]
        msg_b[at : at + 1, :] = ref[pl.ds(7 - 7 * even, 1), :]


def fill_outer(above, below, outer):
    outer[...] = jnp.zeros_like(outer)
    for plane in range(PLANES):
        outer[plane, 0:2, :] = above[2 * plane : 2 * plane + 2]
        outer[plane, 6:8, :] = below[2 * plane : 2 * plane + 2]
    for plane in range(PLANES, PLANES + OLD):
        outer[plane, 0:1, :] = above[PLANES + plane : PLANES + plane + 1]
        outer[plane, 7:8, :] = below[PLANES + plane : PLANES + plane + 1]


def first_edges_kernel(got_a, vel, old_lm, old_mm, own_edges, edges, wide, outer):
    def tile(field, z):
        return vel[field, z] if field < 3 else (old_lm, old_mm)[field - 3][z]

    own_edges[...] = packed_edges(tile)
    wide[0:ROWS, :] = own_edges[...]
    wide[ROWS:, :] = jnp.zeros_like(wide[ROWS:, :])
    fill_outer(got_a[...], got_a[...], outer)
    rows = packed_edges(lambda field, z: outer[LEVELS * field + z], HALF)
    edges[...] = jnp.where(lanes() < HALF, own_edges[...], rows)


def rows_kernel(got_a, got_b, own_edges, outer, edges):
    even = lax.axis_index("gy") % 2 == 0
    above = jnp.where(even, got_a[...], got_b[...])
    below = jnp.where(even, got_b[...], got_a[...])
    fill_outer(above, below, outer)
    rows = packed_edges(lambda field, z: outer[LEVELS * field + z], HALF)
    edges[...] = jnp.where(lanes() < HALF, own_edges[...], rows)


class Grid:
    def __init__(self, shape=(LEVELS, ROWS, COLS)):
        self.rows = len(shape) - 2
        row = lax.broadcasted_iota(jnp.int32, shape, self.rows)
        self.row_first, self.row_last = row == 0, row == ROWS - 1
        self.level = self.levels(shape)

    def levels(self, shape):
        return lax.broadcasted_iota(jnp.int32, shape, 0)

    def east(self, tile):
        return pltpu.roll(tile, COLS - 1, self.rows + 1)

    def west(self, tile):
        return pltpu.roll(tile, 1, self.rows + 1)

    def north(self, here, other):
        return pltpu.roll(jnp.where(self.row_first, other, here), ROWS - 1, self.rows)

    def south(self, here, other):
        return pltpu.roll(jnp.where(self.row_last, other, here), 1, self.rows)

    def twice_slope(self, field):
        inner = (field[2:] - field[:-2]) * (1.0 / spacing_z)
        bottom = (field[1:2] - field[0:1]) * (2.0 / spacing_z)
        top = (field[-1:] - field[-2:-1]) * (2.0 / spacing_z)
        return jnp.concatenate([bottom, inner, top], axis=0)

    def nine(self, own, rows):
        three = (self.south(own, rows), own, self.north(own, rows))
        return [(self.west(t), t, self.east(t)) for t in three]

    def by_level(self, own, rows):
        here = self.nine(own, rows)
        down = [[jnp.concatenate([t[:1], t[:-1]], axis=0) for t in row] for row in here]
        up = [[jnp.concatenate([t[1:], t[-1:]], axis=0) for t in row] for row in here]
        return down, here, up


class EdgeGrid(Grid):
    def __init__(self):
        super().__init__((ROWS, COLS))

    def levels(self, shape):
        return lanes() // GROUP

    def above(self, tile):
        return pltpu.roll(tile, COLS - GROUP, 1)

    def below(self, tile):
        return pltpu.roll(tile, GROUP, 1)

    def twice_slope(self, field):
        bottom, top = self.level == 0, self.level == LEVELS - 1
        high = jnp.where(top, field, self.above(field))
        low = jnp.where(bottom, field, self.below(field))
        return (high - low) * jnp.where(bottom | top, 2.0 / spacing_z, 1.0 / spacing_z)

    def by_level(self, own, rows):
        return (
            self.nine(self.below(own), self.below(rows)),
            self.nine(own, rows),
            self.nine(self.above(own), self.above(rows)),
        )


def spread(low, mid, high):
    return (low + high) + (mid + mid)


def strains(gradient):
    parts = [
        gradient[a][a] if a == b else gradient[b][a] + gradient[a][b]
        for a, b in zip(PAIR_FIRST, PAIR_SECOND)
    ]
    diagonal = parts[0] * parts[0] + parts[1] * parts[1] + parts[2] * parts[2]
    cross = parts[3] * parts[3] + parts[4] * parts[4] + parts[5] * parts[5]
    return parts, jnp.sqrt((diagonal + diagonal) + cross)


def update(grid, fields, offsets, fractions):
    filtered, gradients = [], []
    for own, rows in fields[:3]:
        tiles = (own, rows)
        west = [grid.west(t) for t in tiles]
        east = [grid.east(t) for t in tiles]
        along = [spread(west[t], tiles[t], east[t]) for t in range(2)]
        filtered.append(
            [
                spread(grid.south(along[t], along[1 - t]), along[t], grid.north(along[t], along[1 - t]))
                for t in range(2)
            ]
        )
        gradients.append(
            [
                (
                    east[t] - west[t],
                    grid.north(tiles[t], tiles[1 - t]) - grid.south(tiles[t], tiles[1 - t]),
                    grid.twice_slope(tiles[t]),
                )
                for t in range(2)
            ]
        )
    modelled = []
    for t in range(2):
        parts, magnitude = strains([gradients[c][t] for c in range(3)])
        modelled.append([magnitude * part for part in parts])
    own_f = [filtered[c][0] for c in range(3)]
    parts_f, magnitude_f = strains(
        [
            (
                grid.east(f) - grid.west(f),
                grid.north(f, rows) - grid.south(f, rows),
                grid.twice_slope(f),
            )
            for f, rows in filtered
        ]
    )

    def both_ways(own, rows):
        t = spread(grid.south(own, rows), own, grid.north(own, rows))
        return spread(grid.west(t), t, grid.east(t))

    product_sum = diagonal = cross = 0.0
    for pair, (a, b) in enumerate(zip(PAIR_FIRST, PAIR_SECOND)):
        product = both_ways(fields[a][0] * fields[b][0], fields[a][1] * fields[b][1])
        resolved = 16.0 * product - own_f[a] * own_f[b]
        smooth = both_ways(modelled[0][pair], modelled[1][pair])
        m = 4.0 * smooth - magnitude_f * parts_f[pair]
        product_sum = product_sum + resolved * m
        if a == b:
            diagonal = diagonal + m * m
        else:
            cross = cross + m * m
    scale = 2.0 * filter_area / 256.0
    lm = product_sum * (scale / 256.0)
    mm = (diagonal + 0.5 * cross) * (scale * scale)

    upstream = offsets[0] == 1
    back = offsets[1] == -1
    at_level, one_below = offsets[2] == grid.level, offsets[2] == grid.level - 1
    f0, f1, f2 = fractions
    g0, g1, g2 = 1.0 - f0, 1.0 - f1, 1.0 - f2
    wx = (jnp.where(upstream, g0, 0.0), jnp.where(upstream, f0, g0), jnp.where(upstream, 0.0, f0))
    wy = (jnp.where(back, g1, 0.0), jnp.where(back, f1, g1), jnp.where(back, 0.0, f1))
    wz = (
        jnp.where(one_below, g2, 0.0),
        jnp.where(at_level, g2, jnp.where(one_below, f2, 0.0)),
        jnp.where(at_level, f2, 0.0),
    )
    results = []
    for germano, (own, rows) in ((lm, fields[3]), (mm, fields[4])):
        carried = 0.0
        for weight, nine in zip(wz, grid.by_level(own, rows)):
            plane = 0.0
            for y in range(3):
                plane = plane + wy[y] * (wx[0] * nine[y][0] + wx[1] * nine[y][1] + wx[2] * nine[y][2])
            carried = carried + weight * plane
        results.append(relax_rate * germano + (1.0 - relax_rate) * carried)
    return results


def inner_kernel(
    vel, old_lm, old_mm, offsets, fractions, outer, new, near, near_rows, near_off, near_frac
):
    fields = [vel[c] for c in range(3)] + [old_lm[...], old_mm[...]]
    fields = [(own, outer[LEVELS * f : LEVELS * (f + 1)]) for f, own in enumerate(fields)]
    new[0], new[1] = update(Grid(), fields, [offsets[k] for k in range(3)], [fractions[k] for k in range(3)])
    for field, (own, rows) in enumerate(fields):
        near[field] = edge_domain(lambda z: own[z])
        near_rows[field] = edge_domain(lambda z: rows[z])
    for k in range(3):
        near_off[k] = edge_domain(lambda z: offsets[k, z])
        near_frac[k] = edge_domain(lambda z: fractions[k, z])


def edge_kernel(
    inner, near, near_rows, near_off, near_frac, from_right, left_a, left_b, new_lm, new_mm, coefficient
):
    place = lanes() % GROUP
    is_right, is_left = (place == 4) | (place == 5), (place == 6) | (place == 7)
    even = lax.axis_index("gy") % 2 == 0
    upper = lax.broadcasted_iota(jnp.int32, (ROWS, COLS), 0) < ROWS // 2
    east = from_right[...]
    first, second = left_a[...], pltpu.roll(left_b[0:ROWS, :], HALF, 1)
    west = (
        first,
        jnp.where(even, jnp.where(upper, first, second), jnp.where(upper, second, first)),
    )
    pairs = [[], []]
    for half, own in enumerate((near, near_rows)):
        for field in range(FIELDS):
            at = HALF * half + (4 * field if field < 3 else 12 + 2 * (field - 3))
            to_right = (4 - at - (2 if field < 3 else 1)) % COLS
            to_left = ((6 if field < 3 else 7) - at) % COLS
            tile = jnp.where(is_left, pltpu.roll(west[half], to_left, 1), own[field])
            pairs[half].append(jnp.where(is_right, pltpu.roll(east, to_right, 1), tile))
    fields = list(zip(*pairs))
    edge = update(EdgeGrid(), fields, [near_off[k] for k in range(3)], [near_frac[k] for k in range(3)])
    lane = lanes()
    for z in range(LEVELS):
        out = []
        for k in range(2):
            low = pltpu.roll(edge[k], (COLS - GROUP * z - 8) % COLS, 1)
            high = pltpu.roll(edge[k], (COLS - 4 - GROUP * z) % COLS, 1)
            out.append(jnp.where(lane < 2, low, jnp.where(lane >= COLS - 2, high, inner[k, z])))
        new_lm[z] = out[0]
        new_mm[z] = out[1]
        coefficient[z] = jnp.maximum(out[0], 0.0) / out[1]


def f32(*shape):
    return jax.ShapeDtypeStruct(shape, jnp.float32)


def i32(*shape):
    return jax.ShapeDtypeStruct(shape, jnp.int32)


def kernel_call(kernel, outs, args, spaces=None, scratch=(), limit=16 * 1024):
    return pl.pallas_call(
        kernel,
        out_shape=outs,
        in_specs=[VMEM] * len(args) if spaces is None else spaces,
        out_specs=[VMEM] * len(outs),
        scratch_shapes=scratch,
        compiler_params=pltpu.CompilerParams(vmem_limit_bytes=limit * 1024),
    )(*args)


def even_pairs(count):
    return [(i, i ^ 1) for i in range(count)]


def odd_pairs(count):
    return [(i, (((i + 1) % count ^ 1) - 1) % count) for i in range(count)]


def body(velocity, old_lm, old_mm, offsets, fractions):
    nx, ny = lax.axis_size("gx"), lax.axis_size("gy")
    rows = 2 * PLANES + OLD
    held = [
        pltpu.VMEM((3, LEVELS, ROWS, COLS), jnp.float32),
        pltpu.VMEM((2, LEVELS, ROWS, COLS), jnp.float32),
    ]
    msg_a, msg_b = kernel_call(
        pack_kernel,
        [f32(rows, COLS), f32(rows, COLS)],
        (velocity, old_lm, old_mm),
        spaces=[HBM] * 3,
        scratch=held + [pltpu.SemaphoreType.DMA((3,))],
        limit=55190,
    )
    got_a = lax.ppermute(msg_a, "gy", even_pairs(ny))
    got_b = lax.ppermute(msg_b, "gy", odd_pairs(ny))
    tile = (ROWS, COLS)
    own_edges, edges, wide = kernel_call(
        first_edges_kernel,
        [f32(*tile), f32(*tile), f32(2 * ROWS, COLS)],
        (got_a, velocity, old_lm, old_mm),
        scratch=[pltpu.VMEM((PLANES + OLD, *tile), jnp.float32)],
    )
    to_east = [(i, (i + 1) % nx) for i in range(nx)]
    left_a = lax.ppermute(edges, "gx", to_east)
    left_b = lax.ppermute(
        wide, ("gx", "gy"), [(i * ny + j, k * ny + m) for i, k in to_east for j, m in odd_pairs(ny)]
    )
    outer, edges = kernel_call(
        rows_kernel, [f32(PLANES + OLD, *tile), f32(*tile)], (got_a, got_b, own_edges)
    )
    from_right = lax.ppermute(edges, "gx", [(k, i) for i, k in to_east])
    inner, near, near_rows, near_off, near_frac = kernel_call(
        inner_kernel,
        [f32(2, LEVELS, *tile), f32(FIELDS, *tile), f32(FIELDS, *tile), i32(3, *tile), f32(3, *tile)],
        (velocity, old_lm, old_mm, offsets, fractions, outer),
    )
    out = f32(LEVELS, *tile)
    return tuple(
        kernel_call(
            edge_kernel,
            [out, out, out],
            (inner, near, near_rows, near_off, near_frac, from_right, left_a, left_b),
        )
    )


def solution(mesh):
    placed = (
        P(None, None, "gy", "gx"),
        P(None, "gy", "gx"),
        P(None, "gy", "gx"),
        P(None, None, "gy", "gx"),
        P(None, None, "gy", "gx"),
    )
    return jax.shard_map(
        body,
        mesh=mesh,
        in_specs=placed,
        out_specs=(P(None, "gy", "gx"), P(None, "gy", "gx"), P(None, "gy", "gx")),
        check_vma=False,
    )
```

```python
import jax
import jax.numpy as jnp
from jax import lax
from jax.experimental import pallas as pl
from jax.experimental.pallas import tpu as pltpu
from jax.sharding import PartitionSpec as P

relax_rate = 0.3
filter_area = 0.63
spacing_z = 0.5
PAIR_FIRST = (0, 1, 2, 0, 0, 1)
PAIR_SECOND = (0, 1, 2, 1, 2, 2)
LEVELS = 4
ROWS = 8
COLS = 128
FIELDS = 5
PLANES = 3 * LEVELS
OLD = 2 * LEVELS
GROUP = 16
VMEM = pl.BlockSpec(memory_space=pltpu.VMEM)
HBM = pl.BlockSpec(memory_space=pltpu.HBM)


def lanes():
    return lax.broadcasted_iota(jnp.int32, (ROWS, COLS), 1)


def packed_edges(tile):
    lane = lanes()
    packed = None
    for z in range(LEVELS):
        for field in range(FIELDS):
            first = GROUP * z + (4 * field if field < 3 else 12 + 2 * (field - 3))
            moved = pltpu.roll(tile(field, z), first + (2 if field < 3 else 1), 1)
            packed = moved if packed is None else jnp.where(lane >= first, moved, packed)
    return packed


def from_right_mask():
    lane = lanes() % GROUP
    return jnp.where(lane < 12, lane % 4, 2 * (lane % 2)) >= 2


def edge_domain(tile):
    lane = lanes()
    inner = lane % GROUP < 6
    packed = None
    for z in range(LEVELS):
        at = GROUP * z
        plane = tile(z)
        moved = jnp.where(inner, pltpu.roll(plane, at + 4, 1), pltpu.roll(plane, at + 8, 1))
        packed = moved if packed is None else jnp.where(lane >= at, moved, packed)
    return packed


def pack_kernel(vel_hbm, lm_hbm, mm_hbm, msg_a, msg_b, vel, old, sems):
    pairs = ((vel_hbm, vel), (lm_hbm, old.at[0]), (mm_hbm, old.at[1]))
    copies = [pltpu.make_async_copy(*pair, sems.at[k]) for k, pair in enumerate(pairs)]
    for copy in copies:
        copy.start()
    even = 1 - lax.axis_index("gy") % 2
    for copy in copies:
        copy.wait()
    for plane in range(PLANES):
        ref = vel.at[plane // LEVELS, plane % LEVELS]
        msg_a[2 * plane : 2 * plane + 2, :] = ref[pl.ds(6 * even, 2), :]
        msg_b[2 * plane : 2 * plane + 2, :] = ref[pl.ds(6 - 6 * even, 2), :]
    for plane in range(OLD):
        ref = old.at[plane // LEVELS, plane % LEVELS]
        at = 2 * PLANES + plane
        msg_a[at : at + 1, :] = ref[pl.ds(7 * even, 1), :]
        msg_b[at : at + 1, :] = ref[pl.ds(7 - 7 * even, 1), :]


def fill_outer(above, below, outer):
    outer[...] = jnp.zeros_like(outer)
    for plane in range(PLANES):
        outer[plane, 0:2, :] = above[2 * plane : 2 * plane + 2]
        outer[plane, 6:8, :] = below[2 * plane : 2 * plane + 2]
    for plane in range(PLANES, PLANES + OLD):
        outer[plane, 0:1, :] = above[PLANES + plane : PLANES + plane + 1]
        outer[plane, 7:8, :] = below[PLANES + plane : PLANES + plane + 1]


def packed_rows(message):
    upper = lax.broadcasted_iota(jnp.int32, (ROWS, COLS), 0) < ROWS // 2

    def tile(field, z):
        group, at, last = (field, 2 * z, 6) if field < 3 else (3, LEVELS * (field - 3) + z, 7)
        rows = message[ROWS * group : ROWS * (group + 1), :]
        return jnp.where(
            upper, pltpu.roll(rows, (ROWS - at) % ROWS, 0), pltpu.roll(rows, (last - at) % ROWS, 0)
        )

    return packed_edges(tile)


def first_edges_kernel(got_a, vel, old_lm, old_mm, edges, wide):
    def tile(field, z):
        return vel[field, z] if field < 3 else (old_lm, old_mm)[field - 3][z]

    own_edges = packed_edges(tile)
    wide[0:ROWS, :] = own_edges
    wide[ROWS:, :] = jnp.zeros_like(wide[ROWS:, :])
    edges[0:ROWS, :] = own_edges
    edges[ROWS:, :] = packed_rows(got_a)


def rows_kernel(got_b, first_edges, edges):
    even = lax.axis_index("gy") % 2 == 0
    upper = lax.broadcasted_iota(jnp.int32, (ROWS, COLS), 0) < ROWS // 2
    a, b = first_edges[ROWS:, :], packed_rows(got_b)
    edges[0:ROWS, :] = first_edges[0:ROWS, :]
    edges[ROWS:, :] = jnp.where(even, jnp.where(upper, a, b), jnp.where(upper, b, a))


def fill_both(got_a, got_b, outer):
    even = lax.axis_index("gy") % 2 == 0
    above = jnp.where(even, got_a[...], got_b[...])
    below = jnp.where(even, got_b[...], got_a[...])
    fill_outer(above, below, outer)


class Grid:
    def __init__(self, shape=(LEVELS, ROWS, COLS)):
        self.rows = len(shape) - 2
        row = lax.broadcasted_iota(jnp.int32, shape, self.rows)
        self.row_first, self.row_last = row == 0, row == ROWS - 1
        self.level = self.levels(shape)

    def levels(self, shape):
        return lax.broadcasted_iota(jnp.int32, shape, 0)

    def east(self, tile):
        return pltpu.roll(tile, COLS - 1, self.rows + 1)

    def west(self, tile):
        return pltpu.roll(tile, 1, self.rows + 1)

    def north(self, here, other):
        return pltpu.roll(jnp.where(self.row_first, other, here), ROWS - 1, self.rows)

    def south(self, here, other):
        return pltpu.roll(jnp.where(self.row_last, other, here), 1, self.rows)

    def twice_slope(self, field):
        inner = (field[2:] - field[:-2]) * (1.0 / spacing_z)
        bottom = (field[1:2] - field[0:1]) * (2.0 / spacing_z)
        top = (field[-1:] - field[-2:-1]) * (2.0 / spacing_z)
        return jnp.concatenate([bottom, inner, top], axis=0)

    def nine(self, own, rows):
        three = (self.south(own, rows), own, self.north(own, rows))
        return [(self.west(t), t, self.east(t)) for t in three]

    def by_level(self, own, rows):
        here = self.nine(own, rows)
        down = [[jnp.concatenate([t[:1], t[:-1]], axis=0) for t in row] for row in here]
        up = [[jnp.concatenate([t[1:], t[-1:]], axis=0) for t in row] for row in here]
        return down, here, up


class EdgeGrid(Grid):
    def __init__(self):
        super().__init__((ROWS, COLS))

    def levels(self, shape):
        return lanes() // GROUP

    def above(self, tile):
        return pltpu.roll(tile, COLS - GROUP, 1)

    def below(self, tile):
        return pltpu.roll(tile, GROUP, 1)

    def twice_slope(self, field):
        bottom, top = self.level == 0, self.level == LEVELS - 1
        high = jnp.where(top, field, self.above(field))
        low = jnp.where(bottom, field, self.below(field))
        return (high - low) * jnp.where(bottom | top, 2.0 / spacing_z, 1.0 / spacing_z)

    def by_level(self, own, rows):
        return (
            self.nine(self.below(own), self.below(rows)),
            self.nine(own, rows),
            self.nine(self.above(own), self.above(rows)),
        )


def spread(low, mid, high):
    return (low + high) + (mid + mid)


def strains(gradient):
    parts = [
        gradient[a][a] if a == b else gradient[b][a] + gradient[a][b]
        for a, b in zip(PAIR_FIRST, PAIR_SECOND)
    ]
    diagonal = parts[0] * parts[0] + parts[1] * parts[1] + parts[2] * parts[2]
    cross = parts[3] * parts[3] + parts[4] * parts[4] + parts[5] * parts[5]
    return parts, jnp.sqrt((diagonal + diagonal) + cross)


def update(grid, fields, offsets, fractions):
    filtered, gradients = [], []
    for own, rows in fields[:3]:
        tiles = (own, rows)
        west = [grid.west(t) for t in tiles]
        east = [grid.east(t) for t in tiles]
        along = [spread(west[t], tiles[t], east[t]) for t in range(2)]
        filtered.append(
            [
                spread(grid.south(along[t], along[1 - t]), along[t], grid.north(along[t], along[1 - t]))
                for t in range(2)
            ]
        )
        gradients.append(
            [
                (
                    east[t] - west[t],
                    grid.north(tiles[t], tiles[1 - t]) - grid.south(tiles[t], tiles[1 - t]),
                    grid.twice_slope(tiles[t]),
                )
                for t in range(2)
            ]
        )
    modelled = []
    for t in range(2):
        parts, magnitude = strains([gradients[c][t] for c in range(3)])
        modelled.append([magnitude * part for part in parts])
    own_f = [filtered[c][0] for c in range(3)]
    parts_f, magnitude_f = strains(
        [
            (
                grid.east(f) - grid.west(f),
                grid.north(f, rows) - grid.south(f, rows),
                grid.twice_slope(f),
            )
            for f, rows in filtered
        ]
    )

    def both_ways(own, rows):
        t = spread(grid.south(own, rows), own, grid.north(own, rows))
        return spread(grid.west(t), t, grid.east(t))

    product_sum = diagonal = cross = 0.0
    for pair, (a, b) in enumerate(zip(PAIR_FIRST, PAIR_SECOND)):
        product = both_ways(fields[a][0] * fields[b][0], fields[a][1] * fields[b][1])
        resolved = 16.0 * product - own_f[a] * own_f[b]
        smooth = both_ways(modelled[0][pair], modelled[1][pair])
        m = 4.0 * smooth - magnitude_f * parts_f[pair]
        product_sum = product_sum + resolved * m
        if a == b:
            diagonal = diagonal + m * m
        else:
            cross = cross + m * m
    scale = 2.0 * filter_area / 256.0
    lm = product_sum * (scale / 256.0)
    mm = (diagonal + 0.5 * cross) * (scale * scale)

    upstream = offsets[0] == 1
    back = offsets[1] == -1
    at_level, one_below = offsets[2] == grid.level, offsets[2] == grid.level - 1
    f0, f1, f2 = fractions
    g0, g1, g2 = 1.0 - f0, 1.0 - f1, 1.0 - f2
    wx = (jnp.where(upstream, g0, 0.0), jnp.where(upstream, f0, g0), jnp.where(upstream, 0.0, f0))
    wy = (jnp.where(back, g1, 0.0), jnp.where(back, f1, g1), jnp.where(back, 0.0, f1))
    wz = (
        jnp.where(one_below, g2, 0.0),
        jnp.where(at_level, g2, jnp.where(one_below, f2, 0.0)),
        jnp.where(at_level, f2, 0.0),
    )
    results = []
    for germano, (own, rows) in ((lm, fields[3]), (mm, fields[4])):
        carried = 0.0
        for weight, nine in zip(wz, grid.by_level(own, rows)):
            plane = 0.0
            for y in range(3):
                plane = plane + wy[y] * (wx[0] * nine[y][0] + wx[1] * nine[y][1] + wx[2] * nine[y][2])
            carried = carried + weight * plane
        results.append(relax_rate * germano + (1.0 - relax_rate) * carried)
    return results


def inner_kernel(
    vel, old_lm, old_mm, offsets, fractions, got_a, got_b, new, near, near_rows, near_off, near_frac, outer
):
    fill_both(got_a, got_b, outer)
    fields = [vel[c] for c in range(3)] + [old_lm[...], old_mm[...]]
    fields = [(own, outer[LEVELS * f : LEVELS * (f + 1)]) for f, own in enumerate(fields)]
    new[0], new[1] = update(Grid(), fields, [offsets[k] for k in range(3)], [fractions[k] for k in range(3)])
    for field, (own, rows) in enumerate(fields):
        near[field] = edge_domain(lambda z: own[z])
        near_rows[field] = edge_domain(lambda z: rows[z])
    for k in range(3):
        near_off[k] = edge_domain(lambda z: offsets[k, z])
        near_frac[k] = edge_domain(lambda z: fractions[k, z])


def edge_kernel(
    inner, near, near_rows, near_off, near_frac, from_right, left_a, left_b, new_lm, new_mm, coefficient
):
    right = from_right_mask()
    place = lanes() % GROUP
    is_right, is_left = (place == 4) | (place == 5), (place == 6) | (place == 7)
    even = lax.axis_index("gy") % 2 == 0
    upper = lax.broadcasted_iota(jnp.int32, (ROWS, COLS), 0) < ROWS // 2
    first, second = left_a[ROWS:, :], left_b[0:ROWS, :]
    corners = jnp.where(even, jnp.where(upper, first, second), jnp.where(upper, second, first))
    from_left = (left_a[0:ROWS, :], corners)
    pairs = [[], []]
    for half, own in enumerate((near, near_rows)):
        halo = jnp.where(right, from_right[half * ROWS : (half + 1) * ROWS, :], from_left[half])
        for field in range(FIELDS):
            first = 4 * field if field < 3 else 12 + 2 * (field - 3)
            to_right = (4 - first - (2 if field < 3 else 1)) % COLS
            to_left = ((6 if field < 3 else 7) - first) % COLS
            tile = jnp.where(is_left, pltpu.roll(halo, to_left, 1), own[field])
            pairs[half].append(jnp.where(is_right, pltpu.roll(halo, to_right, 1), tile))
    fields = list(zip(*pairs))
    edge = update(EdgeGrid(), fields, [near_off[k] for k in range(3)], [near_frac[k] for k in range(3)])
    lane = lanes()
    for z in range(LEVELS):
        out = []
        for k in range(2):
            low = pltpu.roll(edge[k], (COLS - GROUP * z - 8) % COLS, 1)
            high = pltpu.roll(edge[k], (COLS - 4 - GROUP * z) % COLS, 1)
            out.append(jnp.where(lane < 2, low, jnp.where(lane >= COLS - 2, high, inner[k, z])))
        new_lm[z] = out[0]
        new_mm[z] = out[1]
        coefficient[z] = jnp.maximum(out[0], 0.0) / out[1]


def f32(*shape):
    return jax.ShapeDtypeStruct(shape, jnp.float32)


def i32(*shape):
    return jax.ShapeDtypeStruct(shape, jnp.int32)


def kernel_call(kernel, outs, args, spaces=None, scratch=(), limit=16 * 1024):
    return pl.pallas_call(
        kernel,
        out_shape=outs,
        in_specs=[VMEM] * len(args) if spaces is None else spaces,
        out_specs=[VMEM] * len(outs),
        scratch_shapes=scratch,
        compiler_params=pltpu.CompilerParams(vmem_limit_bytes=limit * 1024),
    )(*args)


def even_pairs(count):
    return [(i, i ^ 1) for i in range(count)]


def odd_pairs(count):
    return [(i, (((i + 1) % count ^ 1) - 1) % count) for i in range(count)]


def body(velocity, old_lm, old_mm, offsets, fractions):
    nx, ny = lax.axis_size("gx"), lax.axis_size("gy")
    rows = 2 * PLANES + OLD
    held = [
        pltpu.VMEM((3, LEVELS, ROWS, COLS), jnp.float32),
        pltpu.VMEM((2, LEVELS, ROWS, COLS), jnp.float32),
    ]
    msg_a, msg_b = kernel_call(
        pack_kernel,
        [f32(rows, COLS), f32(rows, COLS)],
        (velocity, old_lm, old_mm),
        spaces=[HBM] * 3,
        scratch=held + [pltpu.SemaphoreType.DMA((3,))],
        limit=55190,
    )
    got_a = lax.ppermute(msg_a, "gy", even_pairs(ny))
    got_b = lax.ppermute(msg_b, "gy", odd_pairs(ny))
    tile = (ROWS, COLS)
    edges, wide = kernel_call(
        first_edges_kernel,
        [f32(2 * ROWS, COLS), f32(3 * ROWS, COLS)],
        (got_a, velocity, old_lm, old_mm),
    )
    to_east = [(i, (i + 1) % nx) for i in range(nx)]
    left_a = lax.ppermute(edges, "gx", to_east)
    left_b = lax.ppermute(
        wide, ("gx", "gy"), [(i * ny + j, k * ny + m) for i, k in to_east for j, m in odd_pairs(ny)]
    )
    whole = [pltpu.VMEM((PLANES + OLD, *tile), jnp.float32)]
    (edges,) = kernel_call(rows_kernel, [f32(2 * ROWS, COLS)], (got_b, edges))
    from_right = lax.ppermute(edges, "gx", [(k, i) for i, k in to_east])
    inner, near, near_rows, near_off, near_frac = kernel_call(
        inner_kernel,
        [f32(2, LEVELS, *tile), f32(FIELDS, *tile), f32(FIELDS, *tile), i32(3, *tile), f32(3, *tile)],
        (velocity, old_lm, old_mm, offsets, fractions, got_a, got_b),
        scratch=whole,
    )
    out = f32(LEVELS, *tile)
    return tuple(
        kernel_call(
            edge_kernel,
            [out, out, out],
            (inner, near, near_rows, near_off, near_frac, from_right, left_a, left_b),
        )
    )


def solution(mesh):
    placed = (
        P(None, None, "gy", "gx"),
        P(None, "gy", "gx"),
        P(None, "gy", "gx"),
        P(None, None, "gy", "gx"),
        P(None, None, "gy", "gx"),
    )
    return jax.shard_map(
        body,
        mesh=mesh,
        in_specs=placed,
        out_specs=(P(None, "gy", "gx"), P(None, "gy", "gx"), P(None, "gy", "gx")),
        check_vma=False,
    )
```

```python
import jax
import jax.numpy as jnp
from jax import lax
from jax.experimental import pallas as pl
from jax.experimental.pallas import tpu as pltpu
from jax.sharding import PartitionSpec as P

relax_rate = 0.3
filter_area = 0.63
spacing_z = 0.5
PAIR_FIRST = (0, 1, 2, 0, 0, 1)
PAIR_SECOND = (0, 1, 2, 1, 2, 2)
LEVELS = 4
ROWS = 8
COLS = 128
FIELDS = 5
PLANES = 3 * LEVELS
OLD = 2 * LEVELS
GROUP = 16
VMEM = pl.BlockSpec(memory_space=pltpu.VMEM)
HBM = pl.BlockSpec(memory_space=pltpu.HBM)


def lanes():
    return lax.broadcasted_iota(jnp.int32, (ROWS, COLS), 1)


def packed_edges(tile):
    lane = lanes()
    packed = None
    for z in range(LEVELS):
        for field in range(FIELDS):
            first = GROUP * z + (4 * field if field < 3 else 12 + 2 * (field - 3))
            moved = pltpu.roll(tile(field, z), first + (2 if field < 3 else 1), 1)
            packed = moved if packed is None else jnp.where(lane >= first, moved, packed)
    return packed


def edge_domain(tile):
    lane = lanes()
    inner = lane % GROUP < 6
    packed = None
    for z in range(LEVELS):
        at = GROUP * z
        plane = tile(z)
        moved = jnp.where(inner, pltpu.roll(plane, at + 4, 1), pltpu.roll(plane, at + 8, 1))
        packed = moved if packed is None else jnp.where(lane >= at, moved, packed)
    return packed


def pack_kernel(vel_hbm, lm_hbm, mm_hbm, msg_a, msg_b, vel, old, sems):
    pairs = ((vel_hbm, vel), (lm_hbm, old.at[0]), (mm_hbm, old.at[1]))
    copies = [pltpu.make_async_copy(*pair, sems.at[k]) for k, pair in enumerate(pairs)]
    for copy in copies:
        copy.start()
    even = 1 - lax.axis_index("gy") % 2
    for copy in copies:
        copy.wait()
    for plane in range(PLANES):
        ref = vel.at[plane // LEVELS, plane % LEVELS]
        msg_a[2 * plane : 2 * plane + 2, :] = ref[pl.ds(6 * even, 2), :]
        msg_b[2 * plane : 2 * plane + 2, :] = ref[pl.ds(6 - 6 * even, 2), :]
    for plane in range(OLD):
        ref = old.at[plane // LEVELS, plane % LEVELS]
        at = 2 * PLANES + plane
        msg_a[at : at + 1, :] = ref[pl.ds(7 * even, 1), :]
        msg_b[at : at + 1, :] = ref[pl.ds(7 - 7 * even, 1), :]


def fill_outer(above, below, outer):
    outer[...] = jnp.zeros_like(outer)
    for plane in range(PLANES):
        outer[plane, 0:2, :] = above[2 * plane : 2 * plane + 2]
        outer[plane, 6:8, :] = below[2 * plane : 2 * plane + 2]
    for plane in range(PLANES, PLANES + OLD):
        outer[plane, 0:1, :] = above[PLANES + plane : PLANES + plane + 1]
        outer[plane, 7:8, :] = below[PLANES + plane : PLANES + plane + 1]


def packed_rows(message):
    upper = lax.broadcasted_iota(jnp.int32, (ROWS, COLS), 0) < ROWS // 2

    def tile(field, z):
        group, at, last = (field, 2 * z, 6) if field < 3 else (3, LEVELS * (field - 3) + z, 7)
        rows = message[ROWS * group : ROWS * (group + 1), :]
        return jnp.where(
            upper, pltpu.roll(rows, (ROWS - at) % ROWS, 0), pltpu.roll(rows, (last - at) % ROWS, 0)
        )

    return packed_edges(tile)


def first_edges_kernel(got_a, vel, old_lm, old_mm, edges, wide):
    def tile(field, z):
        return vel[field, z] if field < 3 else (old_lm, old_mm)[field - 3][z]

    own_edges = packed_edges(tile)
    wide[0:ROWS, :] = own_edges
    wide[ROWS:, :] = jnp.zeros_like(wide[ROWS:, :])
    edges[0:ROWS, :] = own_edges
    edges[ROWS:, :] = packed_rows(got_a)


def rows_kernel(got_b, first_edges, edges):
    even = lax.axis_index("gy") % 2 == 0
    upper = lax.broadcasted_iota(jnp.int32, (ROWS, COLS), 0) < ROWS // 2
    a, b = first_edges[ROWS:, :], packed_rows(got_b)
    edges[0:ROWS, :] = first_edges[0:ROWS, :]
    edges[ROWS:, :] = jnp.where(even, jnp.where(upper, a, b), jnp.where(upper, b, a))


def fill_both(got_a, got_b, outer):
    even = lax.axis_index("gy") % 2 == 0
    above = jnp.where(even, got_a[...], got_b[...])
    below = jnp.where(even, got_b[...], got_a[...])
    fill_outer(above, below, outer)


class Grid:
    def __init__(self, shape=(LEVELS, ROWS, COLS)):
        self.rows = len(shape) - 2
        row = lax.broadcasted_iota(jnp.int32, shape, self.rows)
        self.row_first, self.row_last = row == 0, row == ROWS - 1
        self.level = self.levels(shape)

    def levels(self, shape):
        return lax.broadcasted_iota(jnp.int32, shape, 0)

    def east(self, tile):
        return pltpu.roll(tile, COLS - 1, self.rows + 1)

    def west(self, tile):
        return pltpu.roll(tile, 1, self.rows + 1)

    def north(self, here, other):
        return pltpu.roll(jnp.where(self.row_first, other, here), ROWS - 1, self.rows)

    def south(self, here, other):
        return pltpu.roll(jnp.where(self.row_last, other, here), 1, self.rows)

    def twice_slope(self, field):
        inner = (field[2:] - field[:-2]) * (1.0 / spacing_z)
        bottom = (field[1:2] - field[0:1]) * (2.0 / spacing_z)
        top = (field[-1:] - field[-2:-1]) * (2.0 / spacing_z)
        return jnp.concatenate([bottom, inner, top], axis=0)

    def nine(self, own, rows):
        three = (self.south(own, rows), own, self.north(own, rows))
        return [(self.west(t), t, self.east(t)) for t in three]

    def by_level(self, own, rows):
        here = self.nine(own, rows)
        down = [[jnp.concatenate([t[:1], t[:-1]], axis=0) for t in row] for row in here]
        up = [[jnp.concatenate([t[1:], t[-1:]], axis=0) for t in row] for row in here]
        return down, here, up


class EdgeGrid(Grid):
    def __init__(self):
        super().__init__((ROWS, COLS))

    def levels(self, shape):
        return lanes() // GROUP

    def above(self, tile):
        return pltpu.roll(tile, COLS - GROUP, 1)

    def below(self, tile):
        return pltpu.roll(tile, GROUP, 1)

    def twice_slope(self, field):
        bottom, top = self.level == 0, self.level == LEVELS - 1
        high = jnp.where(top, field, self.above(field))
        low = jnp.where(bottom, field, self.below(field))
        return (high - low) * jnp.where(bottom | top, 2.0 / spacing_z, 1.0 / spacing_z)

    def by_level(self, own, rows):
        return (
            self.nine(self.below(own), self.below(rows)),
            self.nine(own, rows),
            self.nine(self.above(own), self.above(rows)),
        )


def spread(low, mid, high):
    return (low + high) + (mid + mid)


def strains(gradient):
    parts = [
        gradient[a][a] if a == b else gradient[b][a] + gradient[a][b]
        for a, b in zip(PAIR_FIRST, PAIR_SECOND)
    ]
    diagonal = parts[0] * parts[0] + parts[1] * parts[1] + parts[2] * parts[2]
    cross = parts[3] * parts[3] + parts[4] * parts[4] + parts[5] * parts[5]
    return parts, jnp.sqrt((diagonal + diagonal) + cross)


def update(grid, fields, offsets, fractions):
    filtered, gradients = [], []
    for own, rows in fields[:3]:
        tiles = (own, rows)
        west = [grid.west(t) for t in tiles]
        east = [grid.east(t) for t in tiles]
        along = [spread(west[t], tiles[t], east[t]) for t in range(2)]
        filtered.append(
            [
                spread(grid.south(along[t], along[1 - t]), along[t], grid.north(along[t], along[1 - t]))
                for t in range(2)
            ]
        )
        gradients.append(
            [
                (
                    east[t] - west[t],
                    grid.north(tiles[t], tiles[1 - t]) - grid.south(tiles[t], tiles[1 - t]),
                    grid.twice_slope(tiles[t]),
                )
                for t in range(2)
            ]
        )
    modelled = []
    for t in range(2):
        parts, magnitude = strains([gradients[c][t] for c in range(3)])
        modelled.append([magnitude * part for part in parts])
    own_f = [filtered[c][0] for c in range(3)]
    parts_f, magnitude_f = strains(
        [
            (
                grid.east(f) - grid.west(f),
                grid.north(f, rows) - grid.south(f, rows),
                grid.twice_slope(f),
            )
            for f, rows in filtered
        ]
    )

    def both_ways(own, rows):
        t = spread(grid.south(own, rows), own, grid.north(own, rows))
        return spread(grid.west(t), t, grid.east(t))

    product_sum = diagonal = cross = 0.0
    for pair, (a, b) in enumerate(zip(PAIR_FIRST, PAIR_SECOND)):
        product = both_ways(fields[a][0] * fields[b][0], fields[a][1] * fields[b][1])
        resolved = 16.0 * product - own_f[a] * own_f[b]
        smooth = both_ways(modelled[0][pair], modelled[1][pair])
        m = 4.0 * smooth - magnitude_f * parts_f[pair]
        product_sum = product_sum + resolved * m
        if a == b:
            diagonal = diagonal + m * m
        else:
            cross = cross + m * m
    scale = 2.0 * filter_area / 256.0
    lm = product_sum * (scale / 256.0)
    mm = (diagonal + 0.5 * cross) * (scale * scale)

    upstream = offsets[0] == 1
    back = offsets[1] == -1
    at_level, one_below = offsets[2] == grid.level, offsets[2] == grid.level - 1
    f0, f1, f2 = fractions
    g0, g1, g2 = 1.0 - f0, 1.0 - f1, 1.0 - f2
    wx = (jnp.where(upstream, g0, 0.0), jnp.where(upstream, f0, g0), jnp.where(upstream, 0.0, f0))
    wy = (jnp.where(back, g1, 0.0), jnp.where(back, f1, g1), jnp.where(back, 0.0, f1))
    wz = (
        jnp.where(one_below, g2, 0.0),
        jnp.where(at_level, g2, jnp.where(one_below, f2, 0.0)),
        jnp.where(at_level, f2, 0.0),
    )
    results = []
    for germano, (own, rows) in ((lm, fields[3]), (mm, fields[4])):
        carried = 0.0
        for weight, nine in zip(wz, grid.by_level(own, rows)):
            plane = 0.0
            for y in range(3):
                plane = plane + wy[y] * (wx[0] * nine[y][0] + wx[1] * nine[y][1] + wx[2] * nine[y][2])
            carried = carried + weight * plane
        results.append(relax_rate * germano + (1.0 - relax_rate) * carried)
    return results


def inner_kernel(
    vel, old_lm, old_mm, offsets, fractions, got_a, got_b, new, near, near_rows, near_off, near_frac, outer
):
    fill_both(got_a, got_b, outer)
    fields = [vel[c] for c in range(3)] + [old_lm[...], old_mm[...]]
    fields = [(own, outer[LEVELS * f : LEVELS * (f + 1)]) for f, own in enumerate(fields)]
    new[0], new[1] = update(Grid(), fields, [offsets[k] for k in range(3)], [fractions[k] for k in range(3)])
    for field, (own, rows) in enumerate(fields):
        near[field] = edge_domain(lambda z: own[z])
        near_rows[field] = edge_domain(lambda z: rows[z])
    for k in range(3):
        near_off[k] = edge_domain(lambda z: offsets[k, z])
        near_frac[k] = edge_domain(lambda z: fractions[k, z])


def edge_kernel(
    inner, near, near_rows, near_off, near_frac, from_right, left_a, left_b, new_lm, new_mm, coefficient
):
    place = lanes() % GROUP
    is_right, is_left = (place == 4) | (place == 5), (place == 6) | (place == 7)
    even = lax.axis_index("gy") % 2 == 0
    upper = lax.broadcasted_iota(jnp.int32, (ROWS, COLS), 0) < ROWS // 2
    first, second = left_a[ROWS:, :], left_b[0:ROWS, :]
    corners = jnp.where(even, jnp.where(upper, first, second), jnp.where(upper, second, first))
    from_left = (left_a[0:ROWS, :], corners)
    pairs = [[], []]
    for half, own in enumerate((near, near_rows)):
        east, west = from_right[half * ROWS : (half + 1) * ROWS, :], from_left[half]
        for field in range(FIELDS):
            first = 4 * field if field < 3 else 12 + 2 * (field - 3)
            to_right = (4 - first - (2 if field < 3 else 1)) % COLS
            to_left = ((6 if field < 3 else 7) - first) % COLS
            tile = jnp.where(is_left, pltpu.roll(west, to_left, 1), own[field])
            pairs[half].append(jnp.where(is_right, pltpu.roll(east, to_right, 1), tile))
    fields = list(zip(*pairs))
    edge = update(EdgeGrid(), fields, [near_off[k] for k in range(3)], [near_frac[k] for k in range(3)])
    lane = lanes()
    for z in range(LEVELS):
        out = []
        for k in range(2):
            low = pltpu.roll(edge[k], (COLS - GROUP * z - 8) % COLS, 1)
            high = pltpu.roll(edge[k], (COLS - 4 - GROUP * z) % COLS, 1)
            out.append(jnp.where(lane < 2, low, jnp.where(lane >= COLS - 2, high, inner[k, z])))
        new_lm[z] = out[0]
        new_mm[z] = out[1]
        coefficient[z] = jnp.maximum(out[0], 0.0) / out[1]


def f32(*shape):
    return jax.ShapeDtypeStruct(shape, jnp.float32)


def i32(*shape):
    return jax.ShapeDtypeStruct(shape, jnp.int32)


def kernel_call(kernel, outs, args, spaces=None, scratch=(), limit=16 * 1024):
    return pl.pallas_call(
        kernel,
        out_shape=outs,
        in_specs=[VMEM] * len(args) if spaces is None else spaces,
        out_specs=[VMEM] * len(outs),
        scratch_shapes=scratch,
        compiler_params=pltpu.CompilerParams(vmem_limit_bytes=limit * 1024),
    )(*args)


def even_pairs(count):
    return [(i, i ^ 1) for i in range(count)]


def odd_pairs(count):
    return [(i, (((i + 1) % count ^ 1) - 1) % count) for i in range(count)]


def body(velocity, old_lm, old_mm, offsets, fractions):
    nx, ny = lax.axis_size("gx"), lax.axis_size("gy")
    rows = 2 * PLANES + OLD
    held = [
        pltpu.VMEM((3, LEVELS, ROWS, COLS), jnp.float32),
        pltpu.VMEM((2, LEVELS, ROWS, COLS), jnp.float32),
    ]
    msg_a, msg_b = kernel_call(
        pack_kernel,
        [f32(rows, COLS), f32(rows, COLS)],
        (velocity, old_lm, old_mm),
        spaces=[HBM] * 3,
        scratch=held + [pltpu.SemaphoreType.DMA((3,))],
        limit=55190,
    )
    got_a = lax.ppermute(msg_a, "gy", even_pairs(ny))
    got_b = lax.ppermute(msg_b, "gy", odd_pairs(ny))
    tile = (ROWS, COLS)
    edges, wide = kernel_call(
        first_edges_kernel,
        [f32(2 * ROWS, COLS), f32(3 * ROWS, COLS)],
        (got_a, velocity, old_lm, old_mm),
    )
    to_east = [(i, (i + 1) % nx) for i in range(nx)]
    left_a = lax.ppermute(edges, "gx", to_east)
    left_b = lax.ppermute(
        wide, ("gx", "gy"), [(i * ny + j, k * ny + m) for i, k in to_east for j, m in odd_pairs(ny)]
    )
    whole = [pltpu.VMEM((PLANES + OLD, *tile), jnp.float32)]
    (edges,) = kernel_call(rows_kernel, [f32(2 * ROWS, COLS)], (got_b, edges))
    from_right = lax.ppermute(edges, "gx", [(k, i) for i, k in to_east])
    inner, near, near_rows, near_off, near_frac = kernel_call(
        inner_kernel,
        [f32(2, LEVELS, *tile), f32(FIELDS, *tile), f32(FIELDS, *tile), i32(3, *tile), f32(3, *tile)],
        (velocity, old_lm, old_mm, offsets, fractions, got_a, got_b),
        scratch=whole,
    )
    out = f32(LEVELS, *tile)
    return tuple(
        kernel_call(
            edge_kernel,
            [out, out, out],
            (inner, near, near_rows, near_off, near_frac, from_right, left_a, left_b),
        )
    )


def solution(mesh):
    placed = (
        P(None, None, "gy", "gx"),
        P(None, "gy", "gx"),
        P(None, "gy", "gx"),
        P(None, None, "gy", "gx"),
        P(None, None, "gy", "gx"),
    )
    return jax.shard_map(
        body,
        mesh=mesh,
        in_specs=placed,
        out_specs=(P(None, "gy", "gx"), P(None, "gy", "gx"), P(None, "gy", "gx")),
        check_vma=False,
    )
```
